32 devices in a mesh: dp: 2 (over y), row: 4 (over x, core), col: 4 (over z).
Axes of the slice: x: 2, y: 2, z: 4, core: 2. Of those that a mesh axis runs over, the one named last changes fastest.
Arguments:
- hidden_in: bfloat16 [4608, 896], P(('dp', 'col'), 'row'), may hold values from -6 to 6
- norm1_gain: float32 [896], P('row'), may hold values from 0.5 to 1.5
- qkv_weight: bfloat16 [896, 1152], P('row', 'col'), may hold values from -0.1875 to 0.1875
- qkv_bias: bfloat16 [1152], P('col'), may hold values from -3 to 3
- out_weight: bfloat16 [896, 896], P('col', 'row'), may hold values from -0.5 to 0.5
- norm2_gain: float32 [896], P('row'), may hold values from 0.5 to 1.5
- gate_weight: bfloat16 [896, 4864], P('row', 'col'), may hold values from -0.1875 to 0.1875
- up_weight: bfloat16 [896, 4864], P('row', 'col'), may hold values from -0.1875 to 0.1875
- down_weight: bfloat16 [4864, 896], P('col', 'row'), may hold values from -0.125 to 0.125
- seq_lens: int32 [2, 9], P('dp'), may hold values from 1 to 1024, 2304 in all within a row
- out_grad: bfloat16 [4608, 896], P(('dp', 'col'), 'row'), may hold values from -6 to 6
Outputs:
- hidden_out: bfloat16 [4608, 896], P(('dp', 'col'), 'row')
- hidden_grad: float32 [4608, 896], P(('dp', 'col'), 'row')
- norm1_gain_grad: float32 [896], P('row')
- qkv_weight_grad: float32 [896, 1152], P('row', 'col')
- qkv_bias_grad: float32 [1152], P('col')
- out_weight_grad: float32 [896, 896], P('col', 'row')
- norm2_gain_grad: float32 [896], P('row')
- gate_weight_grad: float32 [896, 4864], P('row', 'col')
- up_weight_grad: float32 [896, 4864], P('row', 'col')
- down_weight_grad: float32 [4864, 896], P('col', 'row')
The draws below stay inside these ranges and needn't reach their ends.
Inputs may be any that keep to these rules, and one draw needn't show every extreme that they name: Row i of seq_lens lists in order the lengths of the 9 sequences packed into group i; each row sums to 2304 and its longest is 1024.
All inputs are finite; a program needn't handle non-finite values.
Results may differ from the reference program's by a relative error of at most 0.014.
Values may be sent and summed in bfloat16 or wider, within the bound.
No kernel may reach another device: no remote copies, remote signals or barrier semaphores. Data moves between devices by JAX's collectives and lax.ppermute only.
A program may use at most 128 MiB of HBM per device.

```python
import math
import jax
import jax.numpy as jnp
import numpy as np
from jax import lax

D = 896
HEADS = 14
KV_HEADS = 2
HEAD_DIM = 64
FF = 4864
LMAX = 1024
QKV = 1152
TG = 2304
TOKENS = 4608
NSEQ = 9
N_DP = 2


def block_levels(own_key, shape, pieces, least, largest):
    level, own = 1.0, jax.random.fold_in(own_key, 6)
    for axis_at, parts in pieces:
        draws = jnp.exp(jax.random.uniform(jax.random.fold_in(own, axis_at), (parts,), jnp.float32, least / len(pieces), largest / len(pieces)))
        level = level * jnp.repeat(draws, shape[axis_at] // parts).reshape([-1 if axis == axis_at else 1 for axis in range(len(shape))])
    return level


def length_profile(count, total, most, slope):
    weights = [(1 << 20) // math.isqrt(rank ** slope) + 1 for rank in range(2, count + 1)]
    spare, holding = total - most - (count - 1), [1] * (count - 1)
    while spare > 0:
        candidates = [i for i in range(count - 1) if holding[i] < most]
        mass, remaining = sum([weights[i] for i in candidates]), spare
        for i in candidates:
            extra = min(most - holding[i], max(1, remaining * weights[i] // mass), spare)
            holding[i] = holding[i] + extra
            spare = spare - extra
    return np.array([most] + holding)


def ragged_sizes(own_key, amount, total, most, skew):
    if amount == 2:
        one = jax.random.randint(own_key, (), max(1, total - most), min(most, total - 1) + 1)
        return jnp.stack([one, total - one])
    sizes = jnp.asarray(length_profile(amount, total, most, skew), jnp.int32)
    pairs = (amount - 1) // 2
    source_of, taker = sizes[1:1 + 2 * pairs:2], sizes[2:2 + 2 * pairs:2]
    slack = jnp.minimum(source_of - 1, most - taker)
    passed = jax.random.randint(jax.random.fold_in(own_key, 1), (pairs,), 0, 1 << 20) % (slack + 1)
    sizes = sizes.at[1:1 + 2 * pairs:2].set(source_of - passed).at[2:2 + 2 * pairs:2].set(taker + passed)
    return sizes[jax.random.permutation(jax.random.fold_in(own_key, 2), amount)]


def noise(stream_key, dims, scale, bound, cuts=(), kind=jnp.bfloat16):
    values = jax.random.normal(stream_key, dims, jnp.float32) * scale
    if len(cuts) > 0:
        values = block_levels(stream_key, dims, cuts, -0.22, 0.18) * values
    return jnp.clip(values, min=-bound, max=bound).astype(kind)


def setup_inputs(seed: int = 0) -> dict:
    key_list = jax.random.split(jax.random.key(seed), 12)
    hidden_in = noise(key_list[0], (TOKENS, D), 1.0, 6.0, ((0, 8), (1, 4)))
    norm1_gain = jnp.clip(1.0 + 0.1 * jax.random.normal(key_list[1], (D,), jnp.float32), 0.5, 1.5)
    qkv_weight = noise(key_list[2], (D, QKV), D ** -0.5, 0.1875, ((0, 4), (1, 4)))
    qkv_bias = noise(key_list[3], (QKV,), 0.5, 3.0, ((0, 4),))
    out_weight = noise(key_list[4], (D, D), (D // 8) ** -0.5, 0.5, ((0, 4), (1, 4)))
    norm2_gain = jnp.clip(1.0 + 0.1 * jax.random.normal(key_list[5], (D,), jnp.float32), 0.5, 1.5)
    gate_weight = noise(key_list[6], (D, FF), D ** -0.5, 0.1875, ((0, 4), (1, 4)))
    up_weight = noise(key_list[7], (D, FF), D ** -0.5, 0.1875, ((0, 4), (1, 4)))
    down_weight = noise(key_list[8], (FF, D), (FF // 2) ** -0.5, 0.125, ((0, 4), (1, 4)))
    seq_lens = jax.vmap(lambda own: ragged_sizes(own, NSEQ, TG, LMAX, 2))(jax.random.split(key_list[9], N_DP)).reshape((N_DP, NSEQ)).astype(jnp.int32)
    out_grad = noise(key_list[10], (TOKENS, D), 1.0, 6.0, ((0, 8), (1, 4)))
    return {"hidden_in": hidden_in, "norm1_gain": norm1_gain, "qkv_weight": qkv_weight, "qkv_bias": qkv_bias, "out_weight": out_weight, "norm2_gain": norm2_gain, "gate_weight": gate_weight, "up_weight": up_weight, "down_weight": down_weight, "seq_lens": seq_lens, "out_grad": out_grad}


norm_eps = 1e-06
rope_base = 1000000.0
masked_score = -1e+30
highest = lax.Precision.HIGHEST

@jax.custom_vjp
def low(v):
    return lax.optimization_barrier(v.astype(jnp.bfloat16)).astype(jnp.float32)

@jax.custom_vjp
def low_back(v):
    return v

def low_keep(v):
    return (low(v), None)

def low_pass(kept, grad):
    return (grad,)

def back_keep(v):
    return (v, None)

def back_low(kept, grad):
    return (low(grad),)
low.defvjp(low_keep, low_pass)
low_back.defvjp(back_keep, back_low)

def locate(indices, lengths):
    ends = jnp.cumsum(lengths).astype(jnp.int32)
    starts = (ends - lengths).astype(jnp.int32)
    segment = lax.optimization_barrier(jnp.sum((indices[:, None] >= ends[None, :]).astype(jnp.int32), 1)).astype(jnp.int32)
    chosen = segment[:, None] == jnp.arange(lengths.shape[0], dtype=jnp.int32)[None, :]
    position = (indices - lax.optimization_barrier(jnp.sum(jnp.where(chosen, starts[None, :], 0), 1))).astype(jnp.int32)
    return (segment, position)

def rope_tables(position):
    half = HEAD_DIM // 2
    rates = rope_base ** (-(jnp.arange(half, dtype=jnp.float32) * 2.0) / HEAD_DIM)
    angles = position.astype(jnp.float32)[:, None] * rates[None, :]
    cosine = jnp.cos(angles)
    sine = jnp.sin(angles)
    return (jnp.concatenate([cosine, cosine], -1), jnp.concatenate([sine, sine], -1))

def rotate(values, cosine, sine):
    half = values.shape[-1] // 2
    turned = jnp.concatenate([-values[..., half:], values[..., :half]], -1)
    return values * cosine[:, None, :] + turned * sine[:, None, :]

def rms_norm(values, gain):
    mean_square = lax.optimization_barrier(jnp.mean(values * values, -1, keepdims=True))
    return values * lax.rsqrt(mean_square + norm_eps) * gain

def attend(queries, keys, values, segment):
    block = math.gcd(512, TG)
    group_heads = HEADS // KV_HEADS
    scale = 1.0 / math.sqrt(HEAD_DIM)
    indices = jnp.arange(TG, dtype=jnp.int32)

    def one_block(number):
        start = number * block
        block_queries = lax.dynamic_slice_in_dim(queries, start, block, 0).reshape(block, KV_HEADS, group_heads, HEAD_DIM)
        block_segment = lax.dynamic_slice_in_dim(segment, start, block, 0)
        block_index = start + jnp.arange(block, dtype=jnp.int32)
        scores = jnp.einsum('qgha,kga->ghqk', block_queries, keys, precision=highest) * scale
        scores = low_back(scores)
        allowed = (block_segment[:, None] == segment[None, :]) & (indices[None, :] <= block_index[:, None])
        scores = jnp.where(allowed[None, None], scores, masked_score)
        top = lax.optimization_barrier(jnp.max(scores, -1, keepdims=True))
        raised = jnp.exp(scores - top)
        total = lax.optimization_barrier(jnp.sum(raised, -1, keepdims=True))
        weights = low(raised / total)
        result = jnp.einsum('ghqk,kga->qgha', weights, values, precision=highest)
        return result.reshape(block, HEADS * HEAD_DIM)
    outputs = lax.map(jax.checkpoint(one_block), jnp.arange(TG // block, dtype=jnp.int32))
    return outputs.reshape(TG, HEADS * HEAD_DIM)

def layer(inputs, weights, segment, position):
    first_gain, qkv_matrix, qkv_shift, out_matrix, second_gain, gate_matrix, up_matrix, down_matrix = weights
    query_width = HEADS * HEAD_DIM
    kv_width = KV_HEADS * HEAD_DIM
    normed1 = low(rms_norm(inputs, first_gain))
    projected = low_back(jnp.dot(normed1, qkv_matrix, precision=highest, preferred_element_type=jnp.float32) + qkv_shift)
    cosine, sine = rope_tables(position)
    queries = projected[:, :query_width].reshape(TG, HEADS, HEAD_DIM)
    keys = projected[:, query_width:query_width + kv_width].reshape(TG, KV_HEADS, HEAD_DIM)
    values = projected[:, query_width + kv_width:].reshape(TG, KV_HEADS, HEAD_DIM)
    queries = low(rotate(queries, cosine, sine))
    keys = low(rotate(keys, cosine, sine))
    values = low(values)
    attended = low(low_back(attend(queries, keys, values, segment)))
    middle = inputs + low_back(jnp.dot(attended, out_matrix, precision=highest, preferred_element_type=jnp.float32))
    normed2 = low(rms_norm(middle, second_gain))
    gate = low_back(jnp.dot(normed2, gate_matrix, precision=highest, preferred_element_type=jnp.float32))
    up = low_back(jnp.dot(normed2, up_matrix, precision=highest, preferred_element_type=jnp.float32))
    hidden = low(jax.nn.silu(gate) * up)
    return middle + low_back(jnp.dot(hidden, down_matrix, precision=highest, preferred_element_type=jnp.float32))

def reference(hidden_in, norm1_gain, qkv_weight, qkv_bias, out_weight, norm2_gain, gate_weight, up_weight, down_weight, seq_lens, out_grad):
    params = (norm1_gain.astype(jnp.float32), qkv_weight.astype(jnp.float32), qkv_bias.astype(jnp.float32), out_weight.astype(jnp.float32), norm2_gain.astype(jnp.float32), gate_weight.astype(jnp.float32), up_weight.astype(jnp.float32), down_weight.astype(jnp.float32))
    inputs = hidden_in.astype(jnp.float32).reshape(N_DP, TG, D)
    upstream = out_grad.astype(jnp.float32).reshape(N_DP, TG, D)

    def step(carry, item):
        block_in, block_up, lengths = item
        segment, position = locate(jnp.arange(TG, dtype=jnp.int32), lengths)

        def forward(values, *weights):
            return layer(values, weights, segment, position)
        result, pull = jax.vjp(forward, block_in, *params)
        grads = pull(block_up)
        summed = jax.tree.map(lambda older, newer: older + newer, carry, tuple(grads[1:]))
        return (summed, (result.astype(jnp.bfloat16), grads[0]))
    zeros = tuple((jnp.zeros_like(param) for param in params))
    sums, (outputs, input_grads) = lax.scan(step, zeros, (inputs, upstream, seq_lens))
    return (outputs.reshape(TOKENS, D), input_grads.reshape(TOKENS, D), sums[0], sums[1], sums[2], sums[3], sums[4], sums[5], sums[6], sums[7])
```

```python
import jax
import jax.numpy as jnp
from jax import lax
from jax.sharding import PartitionSpec as P

HEADS = 14
KV_HEADS = 2
HEAD_DIM = 64
REACH = 8


norm_eps = 1e-06
rope_base = 1000000.0
masked_score = -1e30

bf16 = jnp.bfloat16
f32 = jnp.float32


def swap(array, axis, flip):
    count = lax.axis_size(axis)
    return lax.ppermute(array, axis, [(i, i ^ flip) for i in range(count)])


def shifted(array, axis, by):
    count = lax.axis_size(axis)
    pairs = [(i, i + by) for i in range(count) if 0 <= i + by < count]
    return lax.ppermute(array, axis, pairs)


def pick(array, index):
    return lax.dynamic_index_in_dim(array, index, 0, keepdims=False)


def product(left, right):
    return jnp.dot(left, right, preferred_element_type=f32)


def product_t(left, right):
    return lax.dot_general(left, right, (((1,), (1,)), ((), ())), preferred_element_type=f32)


def contract_rows(left, right):
    return lax.dot_general(left, right, (((0,), (0,)), ((), ())), preferred_element_type=f32)


def kept(values):
    return lax.optimization_barrier(values.astype(bf16))


def gather_row(block):
    other = swap(block, "row", 2)
    return [block, swap(block, "row", 1), other, swap(other, "row", 1)]


def scatter_row(blocks):
    near = swap(jnp.concatenate([blocks[1], blocks[3]], 0), "row", 1)
    rows = blocks[0].shape[0]
    mine = blocks[0].astype(f32) + near[:rows].astype(f32)
    away = blocks[2].astype(f32) + near[rows:].astype(f32)
    away = kept(away)
    return kept(mine).astype(f32) + swap(away, "row", 2).astype(f32)


def scatter_col(pieces, place):
    own = pick(pieces, place).astype(f32)
    got = [swap(pick(pieces, place ^ flip), "col", flip).astype(f32) for flip in (3, 2, 1)]
    return (own + got[2]) + (got[1] + got[0])


def over_groups(values):
    low = kept(values)
    if lax.axis_size("dp") == 2:
        return low.astype(f32) + swap(low, "dp", 1).astype(f32)
    return lax.psum(low, "dp").astype(f32)


def exchange_row(blocks):
    return [blocks[0]] + [swap(blocks[k], "row", k) for k in (1, 2, 3)]


def locate(indices, lengths):
    ends = jnp.cumsum(lengths)
    starts = ends - lengths
    segment = jnp.sum((indices[:, None] >= ends[None, :]).astype(jnp.int32), 1)
    chosen = segment[:, None] == jnp.arange(lengths.shape[0], dtype=jnp.int32)[None, :]
    position = indices - jnp.sum(jnp.where(chosen, starts[None, :], 0), 1)
    return (segment, position)


def rope_tables(position):
    half = HEAD_DIM // 2
    rates = rope_base ** (-(jnp.arange(half, dtype=f32) * 2.0) / HEAD_DIM)
    angles = position.astype(f32)[:, None] * rates[None, :]
    cosine = jnp.cos(angles)
    sine = jnp.sin(angles)
    return (jnp.concatenate([cosine, cosine], -1), jnp.concatenate([sine, sine], -1))


def rotate(values, cosine, sine):
    half = values.shape[-1] // 2
    turned = jnp.concatenate([-values[..., half:], values[..., :half]], -1)
    return values * cosine[:, None, :] + turned * sine[:, None, :]


def rotate_back(grads, cosine, sine):
    half = grads.shape[-1] // 2
    moved = grads * sine[:, None, :]
    turned = jnp.concatenate([moved[..., half:], -moved[..., :half]], -1)
    return grads * cosine[:, None, :] + turned


def score_block(group_queries, group_keys, allowed, scale):
    scores = (
        jnp.einsum("qha,ka->hqk", group_queries, group_keys, preferred_element_type=f32) * scale
    )
    return jnp.where(allowed[None], scores, masked_score)


def three_parts(values):
    high = lax.reduce_precision(values, 8, 7)
    rest = values - high
    middle = lax.reduce_precision(rest, 8, 7)
    return [high.astype(bf16), middle.astype(bf16), (rest - middle).astype(bf16)]


def body(
    hidden_in,
    norm1_gain,
    qkv_weight,
    qkv_bias,
    out_weight,
    norm2_gain,
    gate_weight,
    up_weight,
    down_weight,
    seq_lens,
    out_grad,
):
    row_count = lax.axis_size("row")
    col_count = lax.axis_size("col")
    row_place = lax.axis_index("row")
    col_place = lax.axis_index("col")
    quarter, part = hidden_in.shape
    block = quarter // row_count
    width = part * row_count
    lengths = seq_lens[0]
    group_heads = HEADS // KV_HEADS
    scale = HEAD_DIM ** (-0.5)
    query_width = HEADS * HEAD_DIM
    kv_width = KV_HEADS * HEAD_DIM
    qkv_cols = qkv_weight.shape[1]
    out_cols = out_weight.shape[0]
    flips = range(row_count)

    both = jnp.concatenate([hidden_in, out_grad], 1).reshape(row_count, block, 2 * part)
    both = exchange_row([pick(both, row_place ^ k) for k in flips])
    inputs_low = jnp.concatenate([b[:, :part] for b in both], 1)
    upstream_low = jnp.concatenate([b[:, part:] for b in both], 1)
    inputs = inputs_low.astype(f32)
    upstream = upstream_low.astype(f32)

    spare = 16
    first_rows = jnp.concatenate([qkv_weight, out_weight.T], 1)
    bias_row = jnp.pad(qkv_bias[None, :], ((0, spare - 1), (0, out_cols)))
    attn_cols = lax.all_gather(jnp.concatenate([first_rows, bias_row], 0), "col", axis=0)
    attn_block = jnp.concatenate(
        [attn_cols[c, :part, :qkv_cols] for c in range(col_count)]
        + [attn_cols[c, :part, qkv_cols:] for c in range(col_count)],
        1,
    )
    bias = jnp.concatenate([attn_cols[c, part, :qkv_cols] for c in range(col_count)], 0)
    gain_rows = jnp.stack(three_parts(norm1_gain) + three_parts(norm2_gain), 0)
    gain_rows = jnp.pad(gain_rows, ((0, spare - 6), (0, attn_block.shape[1] - part)))
    attn_blocks = gather_row(jnp.concatenate([attn_block, gain_rows], 0))
    qkv_wide = query_width + 2 * kv_width
    qkv_full = jnp.concatenate([b[:part, :qkv_wide] for b in attn_blocks], 0)
    out_full_t = jnp.concatenate([b[:part, qkv_wide:] for b in attn_blocks], 0)
    gains = jnp.concatenate([b[part : part + 6, :part] for b in attn_blocks], 1).astype(f32)
    gain1 = gains[0] + gains[1] + gains[2]
    gain2 = gains[3] + gains[4] + gains[5]

    ff_block = jnp.concatenate([gate_weight, up_weight, down_weight.T], 0)
    ff_blocks = gather_row(ff_block)
    gate_full = jnp.concatenate([b[:part] for b in ff_blocks], 0)
    up_full = jnp.concatenate([b[part : 2 * part] for b in ff_blocks], 0)
    down_full_t = jnp.concatenate([b[2 * part :] for b in ff_blocks], 0)

    upstream_all = lax.all_gather(upstream_low, "col", axis=0, tiled=True)

    scale1 = lax.rsqrt(jnp.mean(inputs * inputs, 1, keepdims=True) + norm_eps)
    normed1 = (inputs * scale1 * gain1).astype(bf16)
    projected = product(normed1, qkv_full) + bias.astype(f32)

    place = col_place * row_count + row_place
    first = place * block
    query_index = first + jnp.arange(block, dtype=jnp.int32)
    query_segment, query_position = locate(query_index, lengths)
    cosine, sine = rope_tables(query_position)
    queries = rotate(
        projected[:, :query_width].reshape(block, HEADS, HEAD_DIM), cosine, sine
    ).astype(bf16)
    keys = rotate(
        projected[:, query_width : query_width + kv_width].reshape(block, KV_HEADS, HEAD_DIM),
        cosine,
        sine,
    )
    values = projected[:, query_width + kv_width :]
    own_pair = jnp.concatenate([keys.reshape(block, kv_width), values], 1).astype(bf16)
    spans = REACH // row_count + 1
    from_cols = jnp.concatenate(
        [own_pair] + [shifted(own_pair, "col", back) for back in range(1, spans)], 0
    )
    pairs = jnp.concatenate(gather_row(from_cols), 0).reshape(
        row_count * spans, block, 2 * kv_width
    )
    window = []
    for hop in range(REACH, -1, -1):
        their_row = (row_place - hop) % row_count
        back = (hop + their_row - row_place) // row_count
        window.append(pick(pairs, (row_place ^ their_row) * spans + back))
    window = jnp.concatenate(window, 0)
    key_index = first - REACH * block + jnp.arange((REACH + 1) * block, dtype=jnp.int32)
    key_segment = locate(key_index, lengths)[0]
    allowed = (
        (key_index[None, :] >= 0)
        & (key_segment[None, :] == query_segment[:, None])
        & (key_index[None, :] <= query_index[:, None])
    )
    attended_parts = []
    log_totals = []
    for group in range(KV_HEADS):
        group_queries = queries[:, group * group_heads : (group + 1) * group_heads]
        group_keys = window[:, group * HEAD_DIM : (group + 1) * HEAD_DIM]
        group_values = window[:, kv_width + group * HEAD_DIM : kv_width + (group + 1) * HEAD_DIM]
        scores = score_block(group_queries, group_keys, allowed, scale)
        top = jnp.max(scores, -1, keepdims=True)
        raised = jnp.exp(scores - top)
        total = jnp.sum(raised, -1, keepdims=True)
        weights = (raised / total).astype(bf16)
        attended_parts.append(
            jnp.einsum("hqk,ka->qha", weights, group_values, preferred_element_type=f32)
        )
        log_totals.append(top + jnp.log(total))
    attended = jnp.concatenate(attended_parts, 1).reshape(block, query_width).astype(bf16)

    middle = inputs + product_t(attended, out_full_t)
    scale2 = lax.rsqrt(jnp.mean(middle * middle, 1, keepdims=True) + norm_eps)
    normed2 = (middle * scale2 * gain2).astype(bf16)
    normed2_all = lax.all_gather(normed2, "col", axis=0, tiled=True)

    gate = product(normed2_all, gate_full)
    up = product(normed2_all, up_full)
    grad_hidden = product(upstream_all, down_full_t)
    sigma = jax.nn.sigmoid(gate)
    hidden = (gate * sigma * up).astype(bf16)
    grad_gate = (grad_hidden * up * sigma * (1.0 + gate * (1.0 - sigma))).astype(bf16)
    grad_up = (grad_hidden * gate * sigma).astype(bf16)
    grad_normed2 = (product_t(grad_gate, gate_full) + product_t(grad_up, up_full)).astype(bf16)
    grad_normed2 = scatter_col(grad_normed2.reshape(col_count, block, width), col_place)

    layer_out = product_t(hidden, down_full_t).astype(bf16)
    layer_out = scatter_col(layer_out.reshape(col_count, block, width), col_place)
    hidden_out = (middle + layer_out).astype(bf16)
    hidden_out = exchange_row([hidden_out[:, k * part : (k + 1) * part] for k in flips])

    def ff_grad(left, right):
        whole = contract_rows(left, right).astype(bf16)
        mine = scatter_row([whole[k * part : (k + 1) * part] for k in flips])
        return over_groups(mine)

    down_grad = ff_grad(upstream_all, hidden).T
    gate_grad = ff_grad(normed2_all, grad_gate)
    up_grad = ff_grad(normed2_all, grad_up)

    gain2_grad = jnp.sum(grad_normed2 * middle * scale2, 0)
    scaled2 = grad_normed2 * gain2
    middle_sum = jnp.sum(scaled2 * middle, 1, keepdims=True)
    grad_middle = upstream + scale2 * scaled2 - middle * (scale2**3 * middle_sum / width)
    middle_low = grad_middle.astype(bf16)
    grad_attended = product(middle_low, out_full_t).astype(bf16)
    out_t_grad = contract_rows(middle_low, attended).astype(bf16)

    grad_heads = grad_attended.reshape(block, HEADS, HEAD_DIM)
    query_grads = []
    key_grads = []
    value_grads = []
    for group in range(KV_HEADS):
        group_queries = queries[:, group * group_heads : (group + 1) * group_heads]
        group_keys = window[:, group * HEAD_DIM : (group + 1) * HEAD_DIM]
        group_values = window[:, kv_width + group * HEAD_DIM : kv_width + (group + 1) * HEAD_DIM]
        group_grads = grad_heads[:, group * group_heads : (group + 1) * group_heads]
        scores = score_block(group_queries, group_keys, allowed, scale)
        probs = jnp.exp(scores - log_totals[group])
        grad_probs = jnp.einsum(
            "qha,ka->hqk", group_grads, group_values, preferred_element_type=f32
        )
        grad_scores = (
            probs * (grad_probs - jnp.sum(probs * grad_probs, -1, keepdims=True))
        ).astype(bf16)
        query_grads.append(
            jnp.einsum("hqk,ka->qha", grad_scores, group_keys, preferred_element_type=f32) * scale
        )
        key_grads.append(
            jnp.einsum("hqk,qha->ka", grad_scores, group_queries, preferred_element_type=f32)
            * scale
        )
        value_grads.append(
            jnp.einsum("hqk,qha->ka", probs.astype(bf16), group_grads, preferred_element_type=f32)
        )
    grad_window = jnp.concatenate(key_grads + value_grads, 1).astype(bf16)
    grad_window = grad_window.reshape(REACH + 1, block, 2 * kv_width)
    grad_blocks = []
    for flip in flips:
        pieces = []
        for back in range(spans):
            hop = back * row_count + row_place - (row_place ^ flip)
            inside = (hop >= 0) & (hop <= REACH)
            piece = pick(grad_window, jnp.clip(REACH - hop, 0, REACH))
            pieces.append(jnp.where(inside, piece, jnp.zeros_like(piece)))
        grad_blocks.append(jnp.concatenate(pieces, 0))
    grad_pairs = scatter_row(grad_blocks).reshape(spans, block, 2 * kv_width)
    grad_pair = grad_pairs[0]
    for back in range(1, spans):
        grad_pair = grad_pair + shifted(kept(grad_pairs[back]), "col", -back).astype(f32)

    grad_queries = rotate_back(jnp.concatenate(query_grads, 1), cosine, sine)
    grad_keys = rotate_back(
        grad_pair[:, :kv_width].reshape(block, KV_HEADS, HEAD_DIM), cosine, sine
    )
    grad_projected = jnp.concatenate(
        [
            grad_queries.reshape(block, query_width),
            grad_keys.reshape(block, kv_width),
            grad_pair[:, kv_width:],
        ],
        1,
    ).astype(bf16)
    grad_normed1 = product_t(grad_projected, qkv_full)
    gain1_grad = jnp.sum(grad_normed1 * inputs * scale1, 0)
    scaled1 = grad_normed1 * gain1
    input_sum = jnp.sum(scaled1 * inputs, 1, keepdims=True)
    hidden_grad = grad_middle + scale1 * scaled1 - inputs * (scale1**3 * input_sum / width)
    hidden_grad = exchange_row([hidden_grad[:, k * part : (k + 1) * part] for k in flips])

    out_mine = scatter_row([out_t_grad[k * part : (k + 1) * part] for k in flips])
    out_mine = kept(out_mine).reshape(part, col_count, out_cols).swapaxes(0, 1)
    out_w_grad = over_groups(scatter_col(out_mine, col_place)).T

    qkv_grad = contract_rows(normed1, grad_projected).astype(bf16)
    bias_sums = jnp.sum(grad_projected.astype(f32), 0)
    qkv_blocks = []
    for k in flips:
        extra = [bias_sums]
        for sums in (gain1_grad, gain2_grad):
            sums = jnp.pad(sums[k * part : (k + 1) * part], (0, qkv_cols - part))
            extra.append(jnp.tile(sums, col_count))
        extra = jnp.pad(jnp.stack(extra, 0), ((0, spare - len(extra)), (0, 0))).astype(bf16)
        qkv_blocks.append(jnp.concatenate([qkv_grad[k * part : (k + 1) * part], extra], 0))
    qkv_mine = scatter_row(qkv_blocks)
    qkv_mine = kept(qkv_mine).reshape(part + spare, col_count, qkv_cols).swapaxes(0, 1)
    qkv_mine = over_groups(scatter_col(qkv_mine, col_place))

    return (
        jnp.concatenate(_in_order(hidden_out, row_place), 0),
        jnp.concatenate(_in_order(hidden_grad, row_place), 0),
        qkv_mine[part + 1, :part],
        qkv_mine[:part],
        qkv_mine[part],
        out_w_grad,
        qkv_mine[part + 2, :part],
        gate_grad,
        up_grad,
        down_grad,
    )


def _in_order(blocks, place):
    stacked = jnp.stack(blocks, 0)
    return [pick(stacked, place ^ k) for k in range(len(blocks))]


def solution(mesh):
    return jax.shard_map(
        body,
        mesh=mesh,
        in_specs=(
            P(("dp", "col"), "row"),
            P("row"),
            P("row", "col"),
            P("col"),
            P("col", "row"),
            P("row"),
            P("row", "col"),
            P("row", "col"),
            P("col", "row"),
            P("dp", None),
            P(("dp", "col"), "row"),
        ),
        out_specs=(
            P(("dp", "col"), "row"),
            P(("dp", "col"), "row"),
            P("row"),
            P("row", "col"),
            P("col"),
            P("col", "row"),
            P("row"),
            P("row", "col"),
            P("row", "col"),
            P("col", "row"),
        ),
        check_vma=False,
    )
```

```python
import jax
import jax.numpy as jnp
from jax import lax
from jax.experimental import pallas as pl
from jax.experimental.pallas import tpu as pltpu
from jax.sharding import PartitionSpec as P

HEADS = 14
KV_HEADS = 2
HEAD_DIM = 64
REACH = 8


norm_eps = 1e-06
rope_base = 1000000.0
masked_score = -1e30

bf16 = jnp.bfloat16
f32 = jnp.float32


def swap(array, axis, flip):
    count = lax.axis_size(axis)
    return lax.ppermute(array, axis, [(i, i ^ flip) for i in range(count)])


def shifted(array, axis, by):
    count = lax.axis_size(axis)
    pairs = [(i, i + by) for i in range(count) if 0 <= i + by < count]
    return lax.ppermute(array, axis, pairs)


def pick(array, index):
    return lax.dynamic_index_in_dim(array, index, 0, keepdims=False)


def after(array, *others):
    def kernel(*refs):
        pass

    whole = pl.BlockSpec(memory_space=pl.ANY)
    return pl.pallas_call(
        kernel,
        out_shape=jax.ShapeDtypeStruct(array.shape, array.dtype),
        in_specs=[whole] * (1 + len(others)),
        out_specs=whole,
        input_output_aliases={0: 0},
        cost_estimate=pl.CostEstimate(flops=0, bytes_accessed=0, transcendentals=0),
    )(array, *others)


def kept(values):
    return lax.optimization_barrier(values.astype(bf16))


def gather_col(block):
    far, next_far, near = [swap(block, "col", k) for k in (3, 2, 1)]
    return [block, near, next_far, far]


def gather_row(block):
    other = swap(block, "row", 2)
    return [block, swap(block, "row", 1), other, swap(other, "row", 1)]


def exchange_col(blocks):
    far, next_far, near = [swap(blocks[k], "col", k) for k in (3, 2, 1)]
    return [blocks[0], near, next_far, far]


def add_pieces(pieces):
    a, b, c, d = [p.astype(f32) for p in pieces]
    return (a + b) + (c + d)


def scatter_far(mine, away):
    return mine.astype(f32) + swap(away, "row", 2).astype(f32)


def over_groups(values, *others):
    low = kept(values)
    if lax.axis_size("dp") == 2:
        come = swap(low, "dp", 1)
        if others:
            come = after(come, *others)
        return low.astype(f32) + come.astype(f32)
    return lax.psum(low, "dp").astype(f32)


def exchange_row(blocks):
    return [blocks[0]] + [swap(blocks[k], "row", k) for k in (1, 2, 3)]


def locate(indices, lengths):
    ends = jnp.cumsum(lengths)
    starts = ends - lengths
    segment = jnp.sum((indices[:, None] >= ends[None, :]).astype(jnp.int32), 1)
    chosen = segment[:, None] == jnp.arange(lengths.shape[0], dtype=jnp.int32)[None, :]
    position = indices - jnp.sum(jnp.where(chosen, starts[None, :], 0), 1)
    return (segment, position)


def rope_tables(position):
    half = HEAD_DIM // 2
    rates = rope_base ** (-(jnp.arange(half, dtype=f32) * 2.0) / HEAD_DIM)
    angles = position.astype(f32)[:, None] * rates[None, :]
    cosine = jnp.cos(angles)
    sine = jnp.sin(angles)
    return (jnp.concatenate([cosine, cosine], -1), jnp.concatenate([sine, sine], -1))


def lane_half(shape):
    return lax.broadcasted_iota(jnp.int32, shape, 1) % HEAD_DIM < HEAD_DIM // 2


def lane_roll(values, by):
    by = by % values.shape[1]
    return jnp.concatenate([values[:, -by:], values[:, :-by]], 1)


def turned(values):
    half = HEAD_DIM // 2
    return jnp.where(lane_half(values.shape), -lane_roll(values, -half), lane_roll(values, half))


def turned_back(values):
    half = HEAD_DIM // 2
    return jnp.where(lane_half(values.shape), lane_roll(values, -half), -lane_roll(values, half))


def tiled(table, width):
    return jnp.concatenate([table] * (width // table.shape[1]), 1)


def dot_nt(left, right):
    return lax.dot_general(left, right, (((1,), (1,)), ((), ())), preferred_element_type=f32)


def dot_tn(left, right):
    return lax.dot_general(left, right, (((0,), (0,)), ((), ())), preferred_element_type=f32)


def dot_nn(left, right):
    return jnp.dot(left, right, preferred_element_type=f32)


def flat(ref):
    return ref[...].reshape(-1, ref.shape[-1])


def hop_slot(hop, row_place, row_count):
    their_row = (row_place - hop + 2 * REACH * row_count) % row_count
    return row_place ^ their_row, (hop + their_row - row_place) // row_count


def attend_kernel(
    place_ref, queries_ref, from0, from1, from2, from3, start_ref, inputs_ref, out0, out1, out2, out3, gain_ref,
    attended_ref, window_ref, lse_ref, middle_ref, normed_ref, held, stack, scores,
):
    block = queries_ref.shape[0]
    spans = from0.shape[0] // block
    heads = HEADS // KV_HEADS
    rows = heads * block
    row_place, first = place_ref[0], place_ref[1]
    for flip, ref in enumerate((from0, from1, from2, from3)):
        for back in range(spans):
            held[flip, back] = ref[back * block : (back + 1) * block, :]
    for at in range(REACH + 1):
        flip, back = hop_slot(REACH - at, row_place, 4)
        window_ref[at * block : (at + 1) * block, :] = held[flip, back]
    keys_in = (REACH + 1) * block
    key_index = first - REACH * block + lax.broadcasted_iota(jnp.int32, (block, keys_in), 1)
    query_index = first + lax.broadcasted_iota(jnp.int32, (block, keys_in), 0)
    allowed = (key_index >= start_ref[...]) & (key_index <= query_index)
    bias = jnp.where(allowed, 0.0, masked_score)
    for group in range(KV_HEADS):
        for h in range(heads):
            at = (group * heads + h) * HEAD_DIM
            stack[h * block : (h + 1) * block, :] = queries_ref[:, at : at + HEAD_DIM] * 0.125
        keys = window_ref[:, group * HEAD_DIM : (group + 1) * HEAD_DIM]
        values = window_ref[:, (KV_HEADS + group) * HEAD_DIM : (KV_HEADS + group + 1) * HEAD_DIM]
        scores[...] = dot_nt(stack[...], keys)
        for h in range(heads):
            at = (group * heads + h) * HEAD_DIM
            mine = scores[h * block : (h + 1) * block, :] + bias
            top = jnp.max(mine, 1, keepdims=True)
            raised = jnp.exp(mine - top)
            total = jnp.sum(raised, 1, keepdims=True)
            weights = (raised * (1.0 / total)).astype(bf16)
            attended_ref[:, at : at + HEAD_DIM] = dot_nn(weights, values).astype(bf16)
            lse_ref[group, h * block : (h + 1) * block, :] = top + jnp.log(total)
    attended = attended_ref[...]
    projected = jnp.concatenate([dot_nn(attended, flat(w)) for w in (out0, out1, out2, out3)], 1)
    middle = inputs_ref[...].astype(f32) + projected
    middle_ref[...] = middle
    inv = lax.rsqrt(jnp.mean(middle * middle, 1, keepdims=True) + norm_eps)
    normed_ref[...] = (middle * inv * gain_ref[1:2, :]).astype(bf16)


def attend_back_kernel(
    place_ref, queries_ref, window_ref, start_ref, lse_ref, middle_low_ref, out0, out1, out2, out3, cos_ref, sin_ref,
    query_grad_ref, near_ref, own_ref, stack, outer, scores, probs_grad, low_scores, low_probs, heads_out,
):
    block = queries_ref.shape[0]
    part = out0.shape[-1]
    heads = HEADS // KV_HEADS
    rows = heads * block
    row_place, first = place_ref[0], place_ref[1]
    keys_in = (REACH + 1) * block
    key_index = first - REACH * block + lax.broadcasted_iota(jnp.int32, (block, keys_in), 1)
    query_index = first + lax.broadcasted_iota(jnp.int32, (block, keys_in), 0)
    allowed = (key_index >= start_ref[...]) & (key_index <= query_index)
    bias = jnp.where(allowed, 0.0, masked_score)
    grads = dot_nt(middle_low_ref[:, :part], flat(out0))
    for k, w in enumerate((out1, out2, out3)):
        grads += dot_nt(middle_low_ref[:, (k + 1) * part : (k + 2) * part], flat(w))
    grads = grads.astype(bf16)
    near_ref[...] = jnp.zeros(near_ref.shape, bf16)
    own_ref[...] = jnp.zeros(own_ref.shape, bf16)
    for group in range(KV_HEADS):
        for h in range(heads):
            at = (group * heads + h) * HEAD_DIM
            stack[h * block : (h + 1) * block, :] = queries_ref[:, at : at + HEAD_DIM] * 0.125
            outer[h * block : (h + 1) * block, :] = grads[:, at : at + HEAD_DIM]
        keys = window_ref[:, group * HEAD_DIM : (group + 1) * HEAD_DIM]
        values = window_ref[:, (KV_HEADS + group) * HEAD_DIM : (KV_HEADS + group + 1) * HEAD_DIM]
        scores[...] = dot_nt(stack[...], keys)
        probs_grad[...] = dot_nt(outer[...], values)
        for h in range(heads):
            here = slice(h * block, (h + 1) * block)
            probs = jnp.exp(scores[here, :] + bias - lse_ref[group, here, :])
            moved = probs * probs_grad[here, :]
            total = jnp.sum(moved, 1, keepdims=True)
            low_scores[here, :] = (moved - probs * total).astype(bf16)
            low_probs[here, :] = probs.astype(bf16)
        query_grads = dot_nn(low_scores[...], keys) * 0.125
        for h in range(heads):
            at = (group * heads + h) * HEAD_DIM
            heads_out[:, at : at + HEAD_DIM] = query_grads[h * block : (h + 1) * block, :]
        key_grads = dot_tn(stack[...], low_scores[...]).T.astype(bf16)
        value_grads = dot_tn(outer[...], low_probs[...]).T.astype(bf16)
        for at in range(REACH + 1):
            flip, back = hop_slot(REACH - at, row_place, 4)
            here = slice(at * block, (at + 1) * block)
            key_lanes = slice(group * HEAD_DIM, (group + 1) * HEAD_DIM)
            value_lanes = slice((KV_HEADS + group) * HEAD_DIM, (KV_HEADS + group + 1) * HEAD_DIM)

            @pl.when(flip % 2 == 1)
            def _():
                near_ref[flip // 2, back, :, key_lanes] = key_grads[here, :]
                near_ref[flip // 2, back, :, value_lanes] = value_grads[here, :]

            @pl.when(flip % 2 == 0)
            def _():
                own_ref[flip // 2, back, :, key_lanes] = key_grads[here, :]
                own_ref[flip // 2, back, :, value_lanes] = value_grads[here, :]

    whole = heads_out[...]
    cosine, sine = tiled(cos_ref[...], whole.shape[1]), tiled(sin_ref[...], whole.shape[1])
    query_grad_ref[...] = (whole * cosine + turned_back(whole * sine)).astype(bf16)


def pack_tokens_kernel(place_ref, inputs_ref, upstream_ref, gain1_ref, gain2_ref, *refs):
    outs, tokens = refs[:4], refs[4]
    part, count = inputs_ref.shape
    block = count // 4
    tokens[:, :part] = inputs_ref[...].astype(f32).T.astype(bf16)
    tokens[:, part:] = upstream_ref[...].astype(f32).T.astype(bf16)
    spare = outs[0].shape[0] - block
    rows = []
    for ref in (gain1_ref, gain2_ref):
        rest = ref[...]
        for _ in range(3):
            high = rest.astype(bf16).astype(f32)
            rows.append(high)
            rest = rest - high
    rows.append(jnp.zeros((spare - len(rows), part), f32))
    rows = jnp.concatenate(rows, 0)
    rows = jnp.concatenate([rows, jnp.zeros(rows.shape, f32)], 1).astype(bf16)
    for k, out in enumerate(outs):
        start = pl.multiple_of((place_ref[0] ^ k) * block, 16)
        out[:block, :] = tokens[pl.ds(start, block), :]
        out[block:, :] = rows


def pack_kernel(qkv_ref, bias_ref, out_ref, packed_ref, kept_ref):
    cols, part = qkv_ref.shape
    spare = packed_ref.shape[1] - part
    first = lax.broadcasted_iota(jnp.int32, (cols, spare), 1) == 0
    bias = jnp.where(first, bias_ref[...].astype(f32), 0.0).astype(bf16)
    packed_ref[...] = jnp.concatenate([qkv_ref[...], bias], 1)
    kept_ref[...] = out_ref[...]


def assemble_kernel(place_ref, *refs):
    blocks, out_ref = refs[:4], refs[4]
    for j in range(4):
        out_ref[place_ref[2] ^ j] = blocks[j][...]


def join_upstream_kernel(*refs):
    both, out_ref = refs[:4], refs[4]
    part = both[0].shape[1] // 2
    out_ref[...] = jnp.concatenate([b[:, part:] for b in both], 1)


def pack_feed_kernel(gate_ref, up_ref, down_ref, packed_ref):
    part = gate_ref.shape[0]
    for at, ref in enumerate((gate_ref, up_ref, down_ref)):
        packed_ref[at * part : (at + 1) * part, :] = ref[...]


def add_kernel(own_ref, come_ref, mine_ref, away_ref):
    mine_ref[...] = (own_ref[0].astype(f32) + come_ref[0].astype(f32)).astype(bf16)
    away_ref[...] = (own_ref[1].astype(f32) + come_ref[1].astype(f32)).astype(bf16)


def project_kernel(*refs):
    both, weights = refs[:4], refs[4:8]
    cos_ref, sin_ref = refs[8:10]
    inputs_ref, queries_ref, pair_ref, gains_ref = refs[10:]
    part = both[0].shape[1] // 2
    block = inputs_ref.shape[0]
    spare = weights[0].shape[-1] - part
    inputs_low = jnp.concatenate([b[:block, :part] for b in both], 1)
    inputs_ref[...] = inputs_low
    gains = [b[block : block + 16, :part].astype(f32) for b in both]
    for to in range(2):
        at = 3 * to
        gains_ref[to : to + 1, :] = jnp.concatenate(
            [g[at : at + 1] + g[at + 1 : at + 2] + g[at + 2 : at + 3] for g in gains], 1
        )
    inputs = inputs_low.astype(f32)
    inv = lax.rsqrt(jnp.mean(inputs * inputs, 1, keepdims=True) + norm_eps)
    normed = (inputs * inv * gains_ref[0:1, :]).astype(bf16)
    one = (lax.broadcasted_iota(jnp.int32, (block, spare), 1) == 0).astype(f32).astype(bf16)
    projected = dot_nt(jnp.concatenate([normed[:, :part], one], 1), flat(weights[0]))
    for k in range(1, 4):
        mine = normed[:, k * part : (k + 1) * part]
        projected = projected + dot_nt(
            jnp.concatenate([mine, jnp.zeros_like(one)], 1), flat(weights[k])
        )
    turning = (HEADS + KV_HEADS) * HEAD_DIM
    whole = projected[:, :turning]
    cosine, sine = tiled(cos_ref[...], turning), tiled(sin_ref[...], turning)
    whole = (whole * cosine + turned(whole) * sine).astype(bf16)
    queries_ref[...] = whole[:, : HEADS * HEAD_DIM]
    pair_ref[...] = jnp.concatenate(
        [whole[:, HEADS * HEAD_DIM :], projected[:, turning:].astype(bf16)], 1
    )


def load_blocks(packed, at, part, row_place, into, sems):
    copies = []
    for k in range(4):
        rows = pl.ds(pl.multiple_of((row_place ^ k) * 3 * part + at * part, 16), part)
        copies.append(
            pltpu.make_async_copy(packed.at[rows], into.at[pl.ds(k * part, part)], sems.at[k])
        )
    for copy in copies:
        copy.start()
    return copies


def feed_kernel(place_ref, normed_ref, *refs):
    upstream, packed = refs[0], refs[1]
    normed_grads, layer_ref = refs[2:6], refs[6]
    down_near, down_own, both_near, both_own = refs[7:11]
    gate_w, up_w, down_w, upstream_all, normed_t, upstream_t = refs[11:17]
    hidden, gate_grad, up_grad, grad_hidden, total_ref, sems = refs[17:]
    row_place, col_place = place_ref[0], place_ref[2]
    block, width = normed_grads[0].shape
    part = width // 4
    down_copies = load_blocks(packed, 2, part, row_place, down_w, sems.at[0])
    gate_copies = load_blocks(packed, 0, part, row_place, gate_w, sems.at[1])
    up_copies = load_blocks(packed, 1, part, row_place, up_w, sems.at[2])
    here = [pl.ds(pl.multiple_of((col_place ^ k) * block, 16), block) for k in range(4)]
    for k in range(4):
        upstream_all[k * block : (k + 1) * block, :] = upstream[k, :block, :]
    normed_t[...] = normed_ref[...].astype(f32).T.astype(bf16)
    upstream_t[...] = upstream_all[...].astype(f32).T.astype(bf16)
    cols = hidden.shape[1]
    cuts = [0, 384, 768, cols]
    cuts = [slice(lo, hi) for lo, hi in zip(cuts[:-1], cuts[1:])]
    for copy in down_copies:
        copy.wait()
    for cut in cuts:
        grad_hidden[:, cut] = dot_nn(upstream_all[...], down_w[:, cut])
    for copy in gate_copies + up_copies:
        copy.wait()
    for cut in cuts:
        gate = dot_nn(normed_ref[...], gate_w[:, cut])
        up = dot_nn(normed_ref[...], up_w[:, cut])
        sigma = 1.0 / (1.0 + jnp.exp(-gate))
        silu = gate * sigma
        grad = grad_hidden[:, cut]
        hidden[:, cut] = (silu * up).astype(bf16)
        gate_grad[:, cut] = (grad * up * sigma * (1.0 + gate * (1.0 - sigma))).astype(bf16)
        up_grad[:, cut] = (grad * silu).astype(bf16)
    total_ref[...] = (
        dot_nt(gate_grad[...], gate_w[...]) + dot_nt(up_grad[...], up_w[...])
    ).astype(bf16)
    for k in range(4):
        normed_grads[k][...] = total_ref[here[k], :]
    for left, right, near_ref, own_ref, start in (
        (upstream_t, hidden, down_near, down_own, 0),
        (normed_t, gate_grad, both_near, both_own, 0),
        (normed_t, up_grad, both_near, both_own, part),
    ):
        for cut in cuts:
            whole = dot_nn(left[...], right[:, cut]).astype(bf16)
            for ref, places in ((near_ref, (1, 3)), (own_ref, (0, 2))):
                for at, k in enumerate(places):
                    ref[at, start : start + part, cut] = whole[k * part : (k + 1) * part, :]
    layer_ref[...] = dot_nt(hidden[...], down_w[...]).astype(bf16)


def norm2_back_kernel(*refs):
    pieces, middle_ref, upstream_ref, gains_ref = refs[:4], refs[4], refs[5], refs[6]
    grad_ref, low_ref, sums_ref = refs[-3:]
    grad = (pieces[0][...].astype(f32) + pieces[1][...].astype(f32)) + (
        pieces[2][...].astype(f32) + pieces[3][...].astype(f32)
    )
    middle = middle_ref[...]
    width = middle.shape[1]
    inv = lax.rsqrt(jnp.mean(middle * middle, 1, keepdims=True) + norm_eps)
    sums_ref[...] = jnp.sum(grad * middle * inv, 0, keepdims=True)
    scaled = grad * gains_ref[1:2, :]
    along = jnp.sum(scaled * middle, 1, keepdims=True)
    out = upstream_ref[: middle.shape[0], :].astype(f32) + inv * scaled - middle * (inv * inv * inv * along / width)
    grad_ref[...] = out
    low_ref[...] = out.astype(bf16)


def store_weight_grad(near_ref, own_ref, at, grads, normed):
    part = normed.shape[1] // 4
    spare = near_ref.shape[-1] - part
    ones = jnp.ones((grads.shape[0], spare), f32).astype(bf16)
    blocks = grads.shape[1] // 32
    for ref, places in ((near_ref, (1, 3)), (own_ref, (0, 2))):
        for to, k in enumerate(places):
            mine = jnp.concatenate([normed[:, k * part : (k + 1) * part], ones], 1)
            whole = dot_tn(grads, mine).astype(bf16)
            ref[to, at : at + blocks] = whole.reshape(blocks, 32, part + spare)


def tail_query_kernel(*refs):
    inputs_ref, gains_ref, query_grad_ref, middle_low_ref, attended_ref = refs[:5]
    weights = refs[5:9]
    partial_ref, near_ref, own_ref = refs[9:]
    part = inputs_ref.shape[1] // 4
    grads = query_grad_ref[...]
    cols = grads.shape[1]
    for k in range(4):
        partial_ref[:, k * part : (k + 1) * part] = dot_nn(grads, flat(weights[k])[:cols, :part])
    inputs = inputs_ref[...].astype(f32)
    inv = lax.rsqrt(jnp.mean(inputs * inputs, 1, keepdims=True) + norm_eps)
    normed = (inputs * inv * gains_ref[0:1, :]).astype(bf16)
    store_weight_grad(near_ref, own_ref, 0, grads, normed)
    store_weight_grad(near_ref, own_ref, cols // 32, attended_ref[...], middle_low_ref[...])


def tail_pair_kernel(*refs):
    inputs_ref, gains_ref, middle_grad_ref, partial_ref = refs[:4]
    pair_refs, weights = refs[4:7], refs[7:11]
    sums2_ref, cos_ref, sin_ref = refs[11:14]
    hidden_grads = refs[14:18]
    near_ref, own_ref = refs[18:]
    block, width = inputs_ref.shape
    part = width // 4
    turning = KV_HEADS * HEAD_DIM
    pair = pair_refs[0][...] + pair_refs[1][...].astype(f32) + pair_refs[2][...].astype(f32)
    keys = pair[:, :turning]
    cosine, sine = tiled(cos_ref[...], turning), tiled(sin_ref[...], turning)
    keys = keys * cosine + turned_back(keys * sine)
    grads = jnp.concatenate([keys.astype(bf16), pair[:, turning:].astype(bf16)], 1)
    pair_cols = grads.shape[1]
    grad_normed = [dot_nn(grads, flat(w)[-pair_cols:, :part]) for w in weights]
    grad = partial_ref[...] + jnp.concatenate(grad_normed, 1)
    inputs = inputs_ref[...].astype(f32)
    gain = gains_ref[0:1, :]
    inv = lax.rsqrt(jnp.mean(inputs * inputs, 1, keepdims=True) + norm_eps)
    normed = (inputs * inv * gain).astype(bf16)
    sums1 = jnp.sum(grad * inputs * inv, 0, keepdims=True)
    scaled = grad * gain
    along = jnp.sum(scaled * inputs, 1, keepdims=True)
    out = middle_grad_ref[...] + inv * scaled - inputs * (inv * inv * inv * along / width)
    for k in range(4):
        hidden_grads[k][...] = out[:, k * part : (k + 1) * part]
    store_weight_grad(near_ref, own_ref, 0, grads, normed)
    spare = near_ref.shape[-1] - part
    for ref, places in ((near_ref, (1, 3)), (own_ref, (0, 2))):
        for to, k in enumerate(places):
            here = slice(k * part, (k + 1) * part)
            lines = [sums1[:, here], sums2_ref[:, here], jnp.zeros((30, part), f32)]
            lines = jnp.concatenate(lines, 0)
            lines = jnp.concatenate([lines, jnp.zeros((32, spare), f32)], 1)
            ref[to, pair_cols // 32] = lines.astype(bf16)


def split_kernel(place_ref, mine_ref, come_ref, *refs):
    outs, pieces = refs[:4], refs[4]
    total = (mine_ref[...].astype(f32) + come_ref[...].astype(f32)).astype(bf16)
    count = outs[0].shape[0]
    half = total.shape[0] // 2
    upper, lower = count - half // 4, half // 4
    for c in range(4):
        piece = total[c * upper : min((c + 1) * upper, half)]
        pieces[c, : piece.shape[0]] = piece
        if piece.shape[0] < upper:
            pieces[c, piece.shape[0] : upper] = jnp.zeros((upper - piece.shape[0], *total.shape[1:]), bf16)
        pieces[c, upper:] = total[half + c * lower : half + (c + 1) * lower]
    for j in range(4):
        outs[j][...] = pieces[place_ref[2] ^ j]


VMEM = pl.BlockSpec(memory_space=pltpu.VMEM)
SMEM = pl.BlockSpec(memory_space=pltpu.SMEM)
ANY = pl.BlockSpec(memory_space=pl.ANY)


def call(kernel, outs, operands, specs=None, scratch=(), first=()):
    seen = len(operands)
    specs = list(specs) if specs else [VMEM] * seen

    def run(*refs):
        kernel(*refs[:seen], *refs[seen + len(first) :])

    return pl.pallas_call(
        run,
        out_shape=[jax.ShapeDtypeStruct(shape, dtype) for shape, dtype in outs],
        in_specs=specs + [ANY] * len(first),
        out_specs=[VMEM] * len(outs),
        scratch_shapes=list(scratch),
        cost_estimate=pl.CostEstimate(flops=0, bytes_accessed=0, transcendentals=0),
        compiler_params=pltpu.CompilerParams(vmem_limit_bytes=56 * 2**20),
    )(*operands, *first)


def body(
    hidden_in,
    norm1_gain,
    qkv_weight,
    qkv_bias,
    out_weight,
    norm2_gain,
    gate_weight,
    up_weight,
    down_weight,
    seq_lens,
    out_grad,
):
    row_count = lax.axis_size("row")
    col_count = lax.axis_size("col")
    row_place = lax.axis_index("row")
    col_place = lax.axis_index("col")
    quarter, part = hidden_in.shape
    block = quarter // row_count
    width = part * row_count
    query_width = HEADS * HEAD_DIM
    pair_width = 2 * KV_HEADS * HEAD_DIM
    qkv_cols = qkv_weight.shape[1]
    out_cols = out_weight.shape[0]
    ff_cols = gate_weight.shape[1]
    flips = range(row_count)
    spans = REACH // row_count + 1
    window_rows = (REACH + 1) * block
    group_rows = HEADS // KV_HEADS * block
    spare = 16

    place = col_place * row_count + row_place
    first = place * block
    places = jnp.stack([row_place, first, col_place]).astype(jnp.int32)
    query_index = first + jnp.arange(block, dtype=jnp.int32)
    _, position = locate(query_index, seq_lens[0])
    cosine, sine = [jnp.concatenate([t, t], 1) for t in rope_tables(position)]
    start = (query_index - position)[:, None]

    both = exchange_row(
        call(
            pack_tokens_kernel,
            [((block + spare, 2 * part), bf16)] * 4,
            [places, hidden_in.T, out_grad.T, norm1_gain[None, :], norm2_gain[None, :]],
            [SMEM] + [VMEM] * 4,
            [pltpu.VMEM((quarter, 2 * part), bf16)],
        )
    )

    qkv_packed, out_kept = call(
        pack_kernel,
        [((qkv_cols, part + spare), bf16), (out_weight.shape, bf16)],
        [qkv_weight.T, qkv_bias[:, None], out_weight],
    )

    def whole_cols(block, first=()):
        blocks = gather_col(block)
        return call(
            assemble_kernel,
            [((col_count, *block.shape), bf16)],
            [places, *blocks],
            [SMEM] + [VMEM] * 4,
            (),
            first,
        )[0]

    qkv_block = whole_cols(qkv_packed, [both[2], both[3]])
    qkv_all = gather_row(qkv_block)
    [upstream_low] = call(
        join_upstream_kernel, [((block + spare, width), bf16)], [*both], None, (), [qkv_block]
    )
    out_block = whole_cols(after(out_kept, qkv_block))
    out_blocks = gather_row(after(out_block, qkv_all[2]))
    upstream_all = lax.all_gather(after(upstream_low, out_block), "col", axis=0)

    [ff_packed] = call(
        pack_feed_kernel,
        [((3 * part, ff_cols), bf16)],
        [gate_weight, up_weight, down_weight.T],
        None,
        (),
        [qkv_all[3]],
    )
    ff_all = lax.all_gather(ff_packed, "row", axis=0, tiled=True)

    inputs_low, queries, own_pair, gains = call(
        project_kernel,
        [
            ((block, width), bf16),
            ((block, query_width), bf16),
            ((block, pair_width), bf16),
            ((2, width), f32),
        ],
        [*both, *qkv_all, cosine, sine],
    )

    from_cols = [own_pair] + [shifted(own_pair, "col", back) for back in range(1, spans)]
    from_cols = gather_row(jnp.concatenate(from_cols, 0))
    attended, window, lse, middle, normed2 = call(
        attend_kernel,
        [
            ((block, query_width), bf16),
            ((window_rows, pair_width), bf16),
            ((KV_HEADS, group_rows, 1), f32),
            ((block, width), f32),
            ((block, width), bf16),
        ],
        [places, queries, *from_cols, start, inputs_low, *out_blocks, gains],
        [SMEM] + [VMEM] * 12,
        [
            pltpu.VMEM((row_count, spans, block, pair_width), bf16),
            pltpu.VMEM((group_rows, HEAD_DIM), bf16),
            pltpu.VMEM((group_rows, window_rows), f32),
        ],
    )
    normed2_all = lax.all_gather(normed2, "col", axis=0, tiled=True)

    feed_outs = call(
        feed_kernel,
        [((block, width), bf16)] * 4
        + [((quarter, width), bf16)]
        + [((2, part, ff_cols), bf16)] * 2
        + [((2, 2 * part, ff_cols), bf16)] * 2,
        [places, normed2_all, upstream_all, ff_all],
        [SMEM, VMEM, VMEM, ANY],
        [pltpu.VMEM((width, ff_cols), bf16)] * 3
        + [pltpu.VMEM((quarter, width), bf16)]
        + [pltpu.VMEM((width, quarter), bf16)] * 2
        + [pltpu.VMEM((quarter, ff_cols), bf16)] * 3
        + [pltpu.VMEM((quarter, ff_cols), f32), pltpu.VMEM((quarter, width), bf16)]
        + [pltpu.SemaphoreType.DMA((3, 4))],
    )
    grad_normed2 = exchange_col(feed_outs[:4])

    def near_sum(near, own, first=()):
        return call(
            add_kernel,
            [(own.shape[1:], bf16)] * 2,
            [own, swap(near, "row", 1)],
            None,
            (),
            first,
        )

    down_near = near_sum(feed_outs[5], feed_outs[6])
    both_near = near_sum(feed_outs[7], feed_outs[8], [down_near[1]])
    down_mine = kept(scatter_far(*down_near))
    both_mine = kept(scatter_far(*both_near))

    grad_middle, middle_low, gain2_sums = call(
        norm2_back_kernel,
        [((block, width), f32), ((block, width), bf16), ((1, width), f32)],
        [*grad_normed2, middle, upstream_low, gains],
        None,
        (),
        [down_near[1], both_near[1]],
    )
    layer_out = lax.psum_scatter(
        after(feed_outs[4], middle_low), "col", scatter_dimension=0, tiled=True
    )

    query_grads, pair_near, pair_own = call(
        attend_back_kernel,
        [((block, query_width), bf16)] + [((2, spans, block, pair_width), bf16)] * 2,
        [places, queries, window, start, lse, middle_low, *out_blocks, cosine, sine],
        [SMEM] + [VMEM] * 11,
        [pltpu.VMEM((group_rows, HEAD_DIM), bf16)] * 2
        + [pltpu.VMEM((group_rows, window_rows), f32)] * 2
        + [pltpu.VMEM((group_rows, window_rows), bf16)] * 2
        + [pltpu.VMEM((block, query_width), f32)],
        [down_mine],
    )
    pair_mine, pair_away = near_sum(pair_near, pair_own)
    pair_sums = scatter_far(pair_mine, pair_away)
    pair_back = [shifted(kept(pair_sums[back]), "col", -back) for back in range(1, spans)]

    held = query_width // 32
    partial1, query_near, query_own = call(
        tail_query_kernel,
        [((block, width), f32)] + [((2, 2 * held, 32, part + spare), bf16)] * 2,
        [inputs_low, gains, query_grads, middle_low, attended, *qkv_all],
        None,
        (),
        [pair_away, both_mine],
    )
    query_mine, query_away = near_sum(query_near, query_own)

    *hidden_grad, pair_w_near, pair_w_own = call(
        tail_pair_kernel,
        [((block, part), f32)] * 4 + [((2, pair_width // 32 + 1, 32, part + spare), bf16)] * 2,
        [
            inputs_low,
            gains,
            grad_middle,
            partial1,
            pair_sums[0],
            *pair_back,
            *qkv_all,
            gain2_sums,
            cosine,
            sine,
        ],
        None,
        (),
        [query_away],
    )
    hidden_grad = exchange_row(hidden_grad)
    piece = (qkv_cols // 32 + held // col_count, 32, part + spare)
    query_pieces = call(
        split_kernel,
        [(piece, bf16)] * 4,
        [places, query_mine, swap(query_away, "row", 2)],
        [SMEM, VMEM, VMEM],
        [pltpu.VMEM((4, *piece), bf16)],
    )
    query_pieces = exchange_col(query_pieces)
    pair_w_mine = scatter_far(*near_sum(pair_w_near, pair_w_own, [query_pieces[0]]))
    pair_w_grad = add_pieces(gather_col(kept(pair_w_mine)))
    query_grad = add_pieces(query_pieces)
    query_low = kept(query_grad)
    hidden_grad = [hidden_grad[0]] + [after(b, query_low) for b in hidden_grad[1:]]

    hidden_out = (middle + layer_out.astype(f32)).astype(bf16)
    hidden_out = after(hidden_out, query_low)
    hidden_out = exchange_row([hidden_out[:, k * part : (k + 1) * part] for k in flips])

    down_grad = over_groups(down_mine, pair_w_near).T
    both_grad = over_groups(both_mine, pair_w_near)
    gate_grad, up_grad = both_grad[:part], both_grad[part:]

    cut = qkv_cols // 32
    out_w_grad = over_groups(query_grad[cut:]).reshape(-1, part + spare)[:, :part]
    last = jnp.where(col_place == col_count - 1, 1.0, 0.0)
    pair_blocks = pair_width // 32
    qkv_grad = query_grad[:cut] + last * jnp.pad(
        pair_w_grad[:pair_blocks], ((cut - pair_blocks, 0), (0, 0), (0, 0))
    )
    qkv_grad = over_groups(jnp.concatenate([qkv_grad, pair_w_grad[pair_blocks:]], 0))
    qkv_grad = qkv_grad.reshape(-1, part + spare)

    return (
        jnp.concatenate(_in_order(hidden_out, row_place), 0),
        jnp.concatenate(_in_order(hidden_grad, row_place), 0),
        qkv_grad[qkv_cols, :part],
        qkv_grad[:qkv_cols, :part].T,
        qkv_grad[:qkv_cols, part],
        out_w_grad,
        qkv_grad[qkv_cols + 1, :part],
        gate_grad,
        up_grad,
        down_grad,
    )


def _in_order(blocks, place):
    stacked = jnp.stack(blocks, 0)
    return [pick(stacked, place ^ k) for k in range(len(blocks))]


def solution(mesh):
    return jax.shard_map(
        body,
        mesh=mesh,
        in_specs=(
            P(("dp", "col"), "row"),
            P("row"),
            P("row", "col"),
            P("col"),
            P("col", "row"),
            P("row"),
            P("row", "col"),
            P("row", "col"),
            P("col", "row"),
            P("dp", None),
            P(("dp", "col"), "row"),
        ),
        out_specs=(
            P(("dp", "col"), "row"),
            P(("dp", "col"), "row"),
            P("row"),
            P("row", "col"),
            P("col"),
            P("col", "row"),
            P("row"),
            P("row", "col"),
            P("row", "col"),
            P("col", "row"),
        ),
        check_vma=False,
    )
```

```python
import jax
import jax.numpy as jnp
from jax import lax
from jax.experimental import pallas as pl
from jax.experimental.pallas import tpu as pltpu
from jax.sharding import PartitionSpec as P

HEADS = 14
KV_HEADS = 2
HEAD_DIM = 64
REACH = 8


norm_eps = 1e-06
rope_base = 1000000.0
masked_score = -1e30

bf16 = jnp.bfloat16
f32 = jnp.float32


def swap(array, axis, flip):
    count = lax.axis_size(axis)
    return lax.ppermute(array, axis, [(i, i ^ flip) for i in range(count)])


def shifted(array, axis, by):
    count = lax.axis_size(axis)
    pairs = [(i, i + by) for i in range(count) if 0 <= i + by < count]
    return lax.ppermute(array, axis, pairs)


def pick(array, index):
    return lax.dynamic_index_in_dim(array, index, 0, keepdims=False)


def after(array, *others):
    def kernel(*refs):
        pass

    whole = pl.BlockSpec(memory_space=pl.ANY)
    return pl.pallas_call(
        kernel,
        out_shape=jax.ShapeDtypeStruct(array.shape, array.dtype),
        in_specs=[whole] * (1 + len(others)),
        out_specs=whole,
        input_output_aliases={0: 0},
        cost_estimate=pl.CostEstimate(flops=0, bytes_accessed=0, transcendentals=0),
    )(array, *others)


def all_after(arrays, *others):
    count = len(arrays)

    def kernel(*refs):
        pass

    whole = pl.BlockSpec(memory_space=pl.ANY)
    return pl.pallas_call(
        kernel,
        out_shape=[jax.ShapeDtypeStruct(a.shape, a.dtype) for a in arrays],
        in_specs=[whole] * (count + len(others)),
        out_specs=[whole] * count,
        input_output_aliases={k: k for k in range(count)},
        cost_estimate=pl.CostEstimate(flops=0, bytes_accessed=0, transcendentals=0),
    )(*arrays, *others)


def kept(values):
    return lax.optimization_barrier(values.astype(bf16))


def gather_col(block):
    far, next_far, near = [swap(block, "col", k) for k in (3, 2, 1)]
    return [block, near, next_far, far]


def gather_row(block):
    other = swap(block, "row", 2)
    return [block, swap(block, "row", 1), other, swap(other, "row", 1)]


def exchange_col(blocks):
    far, next_far, near = [swap(blocks[k], "col", k) for k in (3, 2, 1)]
    return [blocks[0], near, next_far, far]


def add_pieces(pieces):
    a, b, c, d = [p.astype(f32) for p in pieces]
    return (a + b) + (c + d)


def scatter_far(mine, away):
    return mine.astype(f32) + swap(away, "row", 2).astype(f32)


def over_groups_start(low):
    if lax.axis_size("dp") == 2:
        return swap(low, "dp", 1)
    return lax.psum(low, "dp")


def over_groups_end(low, come):
    if lax.axis_size("dp") == 2:
        return low.astype(f32) + come.astype(f32)
    return come.astype(f32)


def over_groups(values):
    low = kept(values)
    return over_groups_end(low, over_groups_start(low))


def exchange_row(blocks):
    return [blocks[0]] + [swap(blocks[k], "row", k) for k in (1, 2, 3)]


def locate(indices, lengths):
    ends = jnp.cumsum(lengths)
    starts = ends - lengths
    segment = jnp.sum((indices[:, None] >= ends[None, :]).astype(jnp.int32), 1)
    chosen = segment[:, None] == jnp.arange(lengths.shape[0], dtype=jnp.int32)[None, :]
    position = indices - jnp.sum(jnp.where(chosen, starts[None, :], 0), 1)
    return (segment, position)


def rope_tables(position):
    half = HEAD_DIM // 2
    rates = rope_base ** (-(jnp.arange(half, dtype=f32) * 2.0) / HEAD_DIM)
    angles = position.astype(f32)[:, None] * rates[None, :]
    cosine = jnp.cos(angles)
    sine = jnp.sin(angles)
    return (jnp.concatenate([cosine, cosine], -1), jnp.concatenate([sine, sine], -1))


def lane_half(shape):
    return lax.broadcasted_iota(jnp.int32, shape, 1) % HEAD_DIM < HEAD_DIM // 2


def lane_roll(values, by):
    by = by % values.shape[1]
    return jnp.concatenate([values[:, -by:], values[:, :-by]], 1)


def turned(values):
    half = HEAD_DIM // 2
    return jnp.where(lane_half(values.shape), -lane_roll(values, -half), lane_roll(values, half))


def turned_back(values):
    half = HEAD_DIM // 2
    return jnp.where(lane_half(values.shape), lane_roll(values, -half), -lane_roll(values, half))


def tiled(table, width):
    return jnp.concatenate([table] * (width // table.shape[1]), 1)


def dot_nt(left, right):
    return lax.dot_general(left, right, (((1,), (1,)), ((), ())), preferred_element_type=f32)


def dot_tn(left, right):
    return lax.dot_general(left, right, (((0,), (0,)), ((), ())), preferred_element_type=f32)


def dot_nn(left, right):
    return jnp.dot(left, right, preferred_element_type=f32)


def flat(ref):
    return ref[...].reshape(-1, ref.shape[-1])


def hop_slot(hop, row_place, row_count):
    their_row = (row_place - hop + 2 * REACH * row_count) % row_count
    return row_place ^ their_row, (hop + their_row - row_place) // row_count


def attend_kernel(
    place_ref, queries_ref, from0, from1, from2, from3, start_ref, inputs_ref, out0, out1, out2, out3, gain_ref, attended_ref, window_ref, lse_ref, middle_ref, normed_ref, held, stack, scores,
):
    block = queries_ref.shape[0]
    spans = from0.shape[0] // block
    heads = HEADS // KV_HEADS
    rows = heads * block
    row_place, first = place_ref[0], place_ref[1]
    for flip, ref in enumerate((from0, from1, from2, from3)):
        for back in range(spans):
            held[flip, back] = ref[back * block : (back + 1) * block, :]
    for at in range(REACH + 1):
        flip, back = hop_slot(REACH - at, row_place, 4)
        window_ref[at * block : (at + 1) * block, :] = held[flip, back]
    keys_in = (REACH + 1) * block
    key_index = first - REACH * block + lax.broadcasted_iota(jnp.int32, (block, keys_in), 1)
    query_index = first + lax.broadcasted_iota(jnp.int32, (block, keys_in), 0)
    allowed = (key_index >= start_ref[...]) & (key_index <= query_index)
    bias = jnp.where(allowed, 0.0, masked_score)
    for group in range(KV_HEADS):
        for h in range(heads):
            at = (group * heads + h) * HEAD_DIM
            stack[h * block : (h + 1) * block, :] = queries_ref[:, at : at + HEAD_DIM] * 0.125
        keys = window_ref[:, group * HEAD_DIM : (group + 1) * HEAD_DIM]
        values = window_ref[:, (KV_HEADS + group) * HEAD_DIM : (KV_HEADS + group + 1) * HEAD_DIM]
        scores[...] = dot_nt(stack[...], keys)
        for h in range(heads):
            at = (group * heads + h) * HEAD_DIM
            mine = scores[h * block : (h + 1) * block, :] + bias
            top = jnp.max(mine, 1, keepdims=True)
            raised = jnp.exp(mine - top)
            total = jnp.sum(raised, 1, keepdims=True)
            weights = (raised * (1.0 / total)).astype(bf16)
            attended_ref[:, at : at + HEAD_DIM] = dot_nn(weights, values).astype(bf16)
            lse_ref[group, h * block : (h + 1) * block, :] = top + jnp.log(total)
    attended = attended_ref[...]
    projected = jnp.concatenate(
        [dot_nn(attended, flat(w)) for w in (out0, out1, out2, out3)], 1
    )
    middle = inputs_ref[...].astype(f32) + projected
    middle_ref[...] = middle
    inv = lax.rsqrt(jnp.mean(middle * middle, 1, keepdims=True) + norm_eps)
    normed_ref[...] = (middle * inv * gain_ref[1:2, :]).astype(bf16)


def attend_back_kernel(
    place_ref, queries_ref, window_ref, start_ref, lse_ref, middle_low_ref, out0, out1, out2, out3, cos_ref, sin_ref,
    query_a_ref, query_b_ref, near1_ref, near3_ref, own_ref, stack, outer, scores, probs_grad, low_scores, low_probs, heads_out, near_ref,
):
    block = queries_ref.shape[0]
    part = out0.shape[-1]
    heads = HEADS // KV_HEADS
    rows = heads * block
    row_place, first = place_ref[0], place_ref[1]
    keys_in = (REACH + 1) * block
    key_index = first - REACH * block + lax.broadcasted_iota(jnp.int32, (block, keys_in), 1)
    query_index = first + lax.broadcasted_iota(jnp.int32, (block, keys_in), 0)
    allowed = (key_index >= start_ref[...]) & (key_index <= query_index)
    bias = jnp.where(allowed, 0.0, masked_score)
    grads = dot_nt(middle_low_ref[:, :part], flat(out0))
    for k, w in ((1, out1), (2, out2), (3, out3)):
        grads += dot_nt(middle_low_ref[:, k * part : (k + 1) * part], flat(w))
    grads = grads.astype(bf16)
    near_ref[...] = jnp.zeros(near_ref.shape, bf16)
    own_ref[...] = jnp.zeros(own_ref.shape, bf16)
    for group in range(KV_HEADS):
        for h in range(heads):
            at = (group * heads + h) * HEAD_DIM
            stack[h * block : (h + 1) * block, :] = queries_ref[:, at : at + HEAD_DIM] * 0.125
            outer[h * block : (h + 1) * block, :] = grads[:, at : at + HEAD_DIM]
        keys = window_ref[:, group * HEAD_DIM : (group + 1) * HEAD_DIM]
        values = window_ref[:, (KV_HEADS + group) * HEAD_DIM : (KV_HEADS + group + 1) * HEAD_DIM]
        scores[...] = dot_nt(stack[...], keys)
        probs_grad[...] = dot_nt(outer[...], values)
        for h in range(heads):
            here = slice(h * block, (h + 1) * block)
            probs = jnp.exp(scores[here, :] + bias - lse_ref[group, here, :])
            moved = probs * probs_grad[here, :]
            total = jnp.sum(moved, 1, keepdims=True)
            low_scores[here, :] = (moved - probs * total).astype(bf16)
            low_probs[here, :] = probs.astype(bf16)
        query_grads = dot_nn(low_scores[...], keys) * 0.125
        for h in range(heads):
            at = (group * heads + h) * HEAD_DIM
            heads_out[:, at : at + HEAD_DIM] = query_grads[h * block : (h + 1) * block, :]
        key_grads = dot_tn(stack[...], low_scores[...]).T.astype(bf16)
        value_grads = dot_tn(outer[...], low_probs[...]).T.astype(bf16)
        for at in range(REACH + 1):
            flip, back = hop_slot(REACH - at, row_place, 4)
            here = slice(at * block, (at + 1) * block)
            key_lanes = slice(group * HEAD_DIM, (group + 1) * HEAD_DIM)
            value_lanes = slice((KV_HEADS + group) * HEAD_DIM, (KV_HEADS + group + 1) * HEAD_DIM)

            @pl.when(flip % 2 == 1)
            def _():
                near_ref[flip // 2, back, :, key_lanes] = key_grads[here, :]
                near_ref[flip // 2, back, :, value_lanes] = value_grads[here, :]

            @pl.when(flip % 2 == 0)
            def _():
                own_ref[flip // 2, back, :, key_lanes] = key_grads[here, :]
                own_ref[flip // 2, back, :, value_lanes] = value_grads[here, :]

    near1_ref[...] = near_ref[0]
    near3_ref[...] = near_ref[1]
    whole = heads_out[...]
    cosine, sine = tiled(cos_ref[...], whole.shape[1]), tiled(sin_ref[...], whole.shape[1])
    whole = (whole * cosine + turned_back(whole * sine)).astype(bf16)
    half = query_a_ref.shape[1]
    query_a_ref[...] = whole[:, :half]
    query_b_ref[...] = whole[:, half:]


def other_core(values):
    part = values.shape[1] // 4
    return jnp.concatenate([values[:, part : 2 * part], values[:, 3 * part :]], 1)


def pack_tokens_kernel(place_ref, inputs_ref, upstream_ref, gain1_ref, gain2_ref, *refs):
    outs, tokens = refs[:4], refs[4]
    part, count = inputs_ref.shape
    block = count // 4
    tokens[:, :part] = inputs_ref[...].astype(f32).T.astype(bf16)
    tokens[:, part:] = upstream_ref[...].astype(f32).T.astype(bf16)
    spare = outs[0].shape[0] - block
    rows = []
    for ref in (gain1_ref, gain2_ref):
        rest = ref[...]
        for _ in range(3):
            high = rest.astype(bf16).astype(f32)
            rows.append(high)
            rest = rest - high
    rows.append(jnp.zeros((spare - len(rows), part), f32))
    rows = jnp.concatenate(rows, 0)
    rows = jnp.concatenate([rows, jnp.zeros(rows.shape, f32)], 1).astype(bf16)
    for k, out in enumerate(outs):
        start = pl.multiple_of((place_ref[0] ^ k) * block, 16)
        out[:block, :] = tokens[pl.ds(start, block), :]
        out[block:, :] = rows


def pack_kernel(qkv_ref, bias_ref, out_ref, packed_ref):
    cols, part = qkv_ref.shape
    spare = packed_ref.shape[1] - part
    first = lax.broadcasted_iota(jnp.int32, (cols, spare), 1) == 0
    bias = jnp.where(first, bias_ref[...].astype(f32), 0.0).astype(bf16)
    packed_ref[:cols, :] = jnp.concatenate([qkv_ref[...], bias], 1)
    rows = out_ref.shape[0]
    packed_ref[cols:, :] = jnp.concatenate([out_ref[...], jnp.zeros((rows, spare), bf16)], 1)


def assemble_kernel(place_ref, *refs):
    blocks, outs = refs[:4], refs[4:]
    for j in range(4):
        start = 0
        for out in outs:
            out[place_ref[2] ^ j] = blocks[j][start : start + out.shape[1], : out.shape[2]]
            start += out.shape[1]


def join_upstream_kernel(*refs):
    both, out_ref, again_ref = refs[:4], refs[4], refs[5]
    block = out_ref.shape[0]
    part = both[0].shape[1] // 2
    whole = jnp.concatenate([b[:block, part:] for b in both], 1)
    out_ref[...] = whole
    again_ref[...] = whole


def pack_feed_kernel(gate_ref, up_ref, down_ref, packed_ref):
    part, cols = gate_ref.shape
    for at, ref in enumerate((gate_ref, up_ref, down_ref)):
        packed_ref[at * part : (at + 1) * part, :cols] = ref[...]
    packed_ref[:, cols:] = jnp.zeros((3 * part, packed_ref.shape[1] - cols), bf16)


def add_kernel(own_ref, come_ref, mine_ref, away_ref):
    mine_ref[...] = (own_ref[0].astype(f32) + come_ref[0].astype(f32)).astype(bf16)
    away_ref[...] = (own_ref[1].astype(f32) + come_ref[1].astype(f32)).astype(bf16)


def add_halves_kernel(own_ref, first_ref, second_ref, mine_ref, away_ref):
    mine_ref[...] = (own_ref[0].astype(f32) + first_ref[...].astype(f32)).astype(bf16)
    away_ref[...] = (own_ref[1].astype(f32) + second_ref[...].astype(f32)).astype(bf16)


def project_kernel(*refs):
    both, weights = refs[:4], refs[4:8]
    cos_ref, sin_ref = refs[8:10]
    inputs_ref, queries_ref, pair_ref, gains_ref, other_ref = refs[10:]
    part = both[0].shape[1] // 2
    block = inputs_ref.shape[0]
    spare = weights[0].shape[-1] - part
    inputs_low = jnp.concatenate([b[:block, :part] for b in both], 1)
    inputs_ref[...] = inputs_low
    gains = [b[block : block + 16, :part].astype(f32) for b in both]
    for to in range(2):
        at = 3 * to
        gains_ref[to : to + 1, :] = jnp.concatenate(
            [g[at : at + 1] + g[at + 1 : at + 2] + g[at + 2 : at + 3] for g in gains], 1
        )
    inputs = inputs_low.astype(f32)
    inv = lax.rsqrt(jnp.mean(inputs * inputs, 1, keepdims=True) + norm_eps)
    normed = (inputs * inv * gains_ref[0:1, :]).astype(bf16)
    other_ref[...] = other_core(normed)
    one = (lax.broadcasted_iota(jnp.int32, (block, spare), 1) == 0).astype(f32).astype(bf16)
    projected = dot_nt(jnp.concatenate([normed[:, :part], one], 1), flat(weights[0]))
    for k in range(1, 4):
        mine = normed[:, k * part : (k + 1) * part]
        projected = projected + dot_nt(
            jnp.concatenate([mine, jnp.zeros_like(one)], 1), flat(weights[k])
        )
    turning = (HEADS + KV_HEADS) * HEAD_DIM
    whole = projected[:, :turning]
    cosine, sine = tiled(cos_ref[...], turning), tiled(sin_ref[...], turning)
    whole = (whole * cosine + turned(whole) * sine).astype(bf16)
    queries_ref[...] = whole[:, : HEADS * HEAD_DIM]
    pair_ref[...] = jnp.concatenate(
        [whole[:, HEADS * HEAD_DIM :], projected[:, turning:].astype(bf16)], 1
    )


def load_blocks(packed, at, row_place, into, sems):
    part, cols = into.shape[0] // 4, into.shape[1]
    lanes = pl.ds(pl.multiple_of((row_place % 2) * cols, 128), cols)
    copies = []
    for k in range(4):
        copies.append(
            pltpu.make_async_copy(
                packed[k].at[pl.ds(at * part, part), lanes],
                into.at[pl.ds(k * part, part)],
                sems.at[k],
            )
        )
    for copy in copies:
        copy.start()
    return copies


def other_order(values):
    part = values.shape[1] // 4
    blocks = [values[:, k * part : (k + 1) * part] for k in (1, 0, 3, 2)]
    return jnp.concatenate(blocks, 1)


def feed_kernel(place_ref, normed_ref, normed_other_ref, *refs):
    upstreams, packed, refs = refs[:2], refs[2:6], refs[6:]
    grad_outs, layer_outs, mine_ref, away_ref = refs[:2], refs[2:4], refs[4], refs[5]
    gate_w, up_w, down_w = refs[6:9]
    normed, upstream, normed_t, upstream_t = refs[9:13]
    hidden, gate_grad, up_grad, grad_hidden, sems = refs[13:]
    row_place = place_ref[0]
    down_copies = load_blocks(packed, 2, row_place, down_w, sems.at[0])
    gate_copies = load_blocks(packed, 0, row_place, gate_w, sems.at[1])
    up_copies = load_blocks(packed, 1, row_place, up_w, sems.at[2])
    for at, n_ref in enumerate((normed_ref, normed_other_ref)):
        values = flat(upstreams[at])
        upstream[at] = other_order(values) if at else values
        values = n_ref[...]
        normed[at] = other_order(values) if at else values
        for ref, into_t in ((normed, normed_t), (upstream, upstream_t)):
            into_t[at] = ref[at].astype(f32).T.astype(bf16)
    cols = hidden.shape[2]
    cuts = [slice(lo, min(lo + 384, cols)) for lo in range(0, cols, 384)]
    for copy in down_copies:
        copy.wait()
    for at in range(2):
        for cut in cuts:
            grad_hidden[at, :, cut] = dot_nn(upstream[at], down_w[:, cut])
    for copy in gate_copies + up_copies:
        copy.wait()
    for at in range(2):
        for cut in cuts:
            gate = dot_nn(normed[at], gate_w[:, cut])
            up = dot_nn(normed[at], up_w[:, cut])
            sigma = 1.0 / (1.0 + jnp.exp(-gate))
            silu = gate * sigma
            grad = grad_hidden[at, :, cut]
            hidden[at, :, cut] = (silu * up).astype(bf16)
            gate_grad[at, :, cut] = (
                grad * up * sigma * (1.0 + gate * (1.0 - sigma))
            ).astype(bf16)
            up_grad[at, :, cut] = (grad * silu).astype(bf16)
    for at in range(2):
        total = dot_nt(gate_grad[at], gate_w[...]) + dot_nt(up_grad[at], up_w[...])
        total = total.astype(bf16)
        grad_outs[at][...] = other_order(total) if at else total
        total = dot_nt(hidden[at], down_w[...]).astype(bf16)
        layer_outs[at][...] = other_order(total) if at else total
    part = gate_w.shape[0] // 4
    for to, (left, right) in enumerate(
        ((normed_t, gate_grad), (normed_t, up_grad), (upstream_t, hidden))
    ):
        for cut in cuts:
            whole = dot_nn(left[0], right[0, :, cut]) + dot_nn(left[1], right[1, :, cut])
            whole = whole.astype(bf16)
            mine_ref[to, :, cut] = whole[: 2 * part]
            away_ref[to, :, cut] = whole[2 * part :]


def split_tokens_kernel(place_ref, mine_ref, come_ref, *outs):
    total, outs = outs[-1], outs[:-1]
    total[...] = (mine_ref[...].astype(f32) + come_ref[...].astype(f32)).astype(bf16)
    block = outs[0].shape[0]
    for k in range(4):
        start = pl.multiple_of((place_ref[2] ^ k) * block, 16)
        outs[k][...] = total[pl.ds(start, block), :]


def feed_sum_kernel(mine_ref, come_ref, kept_ref, give_ref):
    part = kept_ref.shape[1]
    total = (mine_ref[...].astype(f32) + come_ref[...].astype(f32)).astype(bf16)
    kept_ref[...] = total[:, :part]
    give_ref[...] = total[:, part:]


def feed_join_kernel(place_ref, mine_ref, come_ref, out_ref, whole):
    cols = mine_ref.shape[2]
    core = place_ref[0] % 2
    whole[:, :, pl.ds(pl.multiple_of(core * cols, 128), cols)] = mine_ref[...]
    whole[:, :, pl.ds(pl.multiple_of((1 - core) * cols, 128), cols)] = come_ref[...]
    out_ref[...] = whole[:, :, : out_ref.shape[2]]


def norm2_back_kernel(*refs):
    pieces, middle_ref, upstream_ref, gains_ref = refs[:4], refs[4], refs[5], refs[6]
    grad_ref, low_ref, sums_ref, other_ref = refs[-4:]
    grad = (pieces[0][...].astype(f32) + pieces[1][...].astype(f32)) + (
        pieces[2][...].astype(f32) + pieces[3][...].astype(f32)
    )
    middle = middle_ref[...]
    width = middle.shape[1]
    inv = lax.rsqrt(jnp.mean(middle * middle, 1, keepdims=True) + norm_eps)
    sums_ref[...] = jnp.sum(grad * middle * inv, 0, keepdims=True)
    scaled = grad * gains_ref[1:2, :]
    along = jnp.sum(scaled * middle, 1, keepdims=True)
    out = upstream_ref[: middle.shape[0], :].astype(f32) + inv * scaled - middle * (inv * inv * inv * along / width)
    grad_ref[...] = out
    low_ref[...] = out.astype(bf16)
    other_ref[...] = other_core(out).astype(bf16)


def store_weight_grad(near_ref, own_ref, at, grads, normed):
    part = normed.shape[1] // 4
    spare = near_ref.shape[-1] - part
    ones = jnp.ones((grads.shape[0], spare), f32).astype(bf16)
    blocks = grads.shape[1] // 32
    for ref, places in ((near_ref, (1, 3)), (own_ref, (0, 2))):
        for to, k in enumerate(places):
            mine = jnp.concatenate([normed[:, k * part : (k + 1) * part], ones], 1)
            whole = dot_tn(grads, mine).astype(bf16)
            ref[to, at : at + blocks] = whole.reshape(blocks, 32, part + spare)


def core_weight_grad(grads, normed, other_grads, other_normed, mine_ref, away_ref):
    part = normed.shape[1] // 4
    spare = mine_ref.shape[-1] - part
    both = jnp.concatenate([grads, other_grads], 0)
    ones = jnp.ones((both.shape[0], spare), f32).astype(bf16)
    for ref, k, at in ((mine_ref, 0, 0), (away_ref, 2, 1)):
        mine = normed[:, k * part : (k + 1) * part]
        other = other_normed[:, at * part : (at + 1) * part]
        mine = jnp.concatenate([jnp.concatenate([mine, other], 0), ones], 1)
        ref[...] = dot_tn(both, mine).astype(bf16).reshape(ref.shape)


def tail_query_kernel(*refs):
    inputs_ref, gains_ref, query_a, query_b, other_normed_ref, other_a, other_b = refs[:7]
    low_ref, attended_ref, other_low_ref, other_attended_ref = refs[7:11]
    weights = refs[11:15]
    partial_ref, mine_ref, away_ref = refs[15:]
    part = inputs_ref.shape[1] // 4
    grads = jnp.concatenate([query_a[...], query_b[...]], 1)
    other_grads = jnp.concatenate([other_a[...], other_b[...]], 1)
    cols = grads.shape[1]
    for k in range(4):
        partial_ref[:, k * part : (k + 1) * part] = dot_nn(grads, flat(weights[k])[:cols, :part])
    inputs = inputs_ref[...].astype(f32)
    inv = lax.rsqrt(jnp.mean(inputs * inputs, 1, keepdims=True) + norm_eps)
    normed = (inputs * inv * gains_ref[0:1, :]).astype(bf16)
    half = mine_ref.shape[0] // 2
    for at, (one, two, three, four) in enumerate(
        (
            (grads, normed, other_grads, other_normed_ref[...]),
            (attended_ref[...], low_ref[...], other_attended_ref[...], other_low_ref[...]),
        )
    ):
        here = pl.ds(at * half, half)
        core_weight_grad(one, two, three, four, mine_ref.at[here], away_ref.at[here])


def tail_pair_kernel(*refs):
    inputs_ref, gains_ref, middle_grad_ref, partial_ref = refs[:4]
    pair_refs, weights = refs[4:7], refs[7:11]
    sums2_ref, cos_ref, sin_ref, middle_ref = refs[11:15]
    layer_refs = refs[15:19]
    results = refs[19:23]
    near_ref, own_ref = refs[23:]
    block, width = inputs_ref.shape
    part = width // 4
    turning = KV_HEADS * HEAD_DIM
    pair = pair_refs[0][...] + pair_refs[1][...].astype(f32) + pair_refs[2][...].astype(f32)
    keys = pair[:, :turning]
    cosine, sine = tiled(cos_ref[...], turning), tiled(sin_ref[...], turning)
    keys = keys * cosine + turned_back(keys * sine)
    grads = jnp.concatenate([keys.astype(bf16), pair[:, turning:].astype(bf16)], 1)
    pair_cols = grads.shape[1]
    grad_normed = [dot_nn(grads, flat(w)[-pair_cols:, :part]) for w in weights]
    grad = partial_ref[...] + jnp.concatenate(grad_normed, 1)
    inputs = inputs_ref[...].astype(f32)
    gain = gains_ref[0:1, :]
    inv = lax.rsqrt(jnp.mean(inputs * inputs, 1, keepdims=True) + norm_eps)
    normed = (inputs * inv * gain).astype(bf16)
    sums1 = jnp.sum(grad * inputs * inv, 0, keepdims=True)
    scaled = grad * gain
    along = jnp.sum(scaled * inputs, 1, keepdims=True)
    out = middle_grad_ref[...] + inv * scaled - inputs * (inv * inv * inv * along / width)
    layer = (layer_refs[0][...].astype(f32) + layer_refs[1][...].astype(f32)) + (
        layer_refs[2][...].astype(f32) + layer_refs[3][...].astype(f32)
    )
    high = out.astype(bf16)
    low = (out - high.astype(f32)).astype(bf16)
    for at, values in enumerate((high, low, (middle_ref[...] + layer).astype(bf16))):
        for k in range(4):
            results[k][at] = values[:, k * part : (k + 1) * part]
    store_weight_grad(near_ref, own_ref, 0, grads, normed)
    spare = near_ref.shape[-1] - part
    for ref, places in ((near_ref, (1, 3)), (own_ref, (0, 2))):
        for to, k in enumerate(places):
            here = slice(k * part, (k + 1) * part)
            lines = [sums1[:, here], sums2_ref[:, here], jnp.zeros((30, part), f32)]
            lines = jnp.concatenate(lines, 0)
            lines = jnp.concatenate([lines, jnp.zeros((32, spare), f32)], 1)
            ref[to, pair_cols // 32] = lines.astype(bf16)


def split_kernel(place_ref, mine_ref, come_ref, *refs):
    outs, pieces = refs[:4], refs[4]
    total = (mine_ref[...].astype(f32) + come_ref[...].astype(f32)).astype(bf16)
    count = outs[0].shape[0]
    half = total.shape[0] // 2
    upper, lower = count - half // 4, half // 4
    for c in range(4):
        piece = total[c * upper : min((c + 1) * upper, half)]
        held = piece.shape[0]
        pieces[c, :held] = piece
        if held < upper:
            pieces[c, held:upper] = jnp.zeros((upper - held, *total.shape[1:]), bf16)
        pieces[c, upper:] = total[half + c * lower : half + (c + 1) * lower]
    for j in range(4):
        outs[j][...] = pieces[place_ref[2] ^ j]


VMEM = pl.BlockSpec(memory_space=pltpu.VMEM)
SMEM = pl.BlockSpec(memory_space=pltpu.SMEM)
ANY = pl.BlockSpec(memory_space=pl.ANY)


def call(kernel, outs, operands, specs=None, scratch=(), first=()):
    seen = len(operands)
    specs = list(specs) if specs else [VMEM] * seen

    def run(*refs):
        kernel(*refs[:seen], *refs[seen + len(first) :])

    return pl.pallas_call(
        run,
        out_shape=[jax.ShapeDtypeStruct(shape, dtype) for shape, dtype in outs],
        in_specs=specs + [ANY] * len(first),
        out_specs=[VMEM] * len(outs),
        scratch_shapes=list(scratch),
        cost_estimate=pl.CostEstimate(flops=0, bytes_accessed=0, transcendentals=0),
        compiler_params=pltpu.CompilerParams(vmem_limit_bytes=56 * 2**20),
    )(*operands, *first)


def body(
    hidden_in,
    norm1_gain,
    qkv_weight,
    qkv_bias,
    out_weight,
    norm2_gain,
    gate_weight,
    up_weight,
    down_weight,
    seq_lens,
    out_grad,
):
    row_count = lax.axis_size("row")
    col_count = lax.axis_size("col")
    row_place = lax.axis_index("row")
    col_place = lax.axis_index("col")
    quarter, part = hidden_in.shape
    block = quarter // row_count
    width = part * row_count
    query_width = HEADS * HEAD_DIM
    pair_width = 2 * KV_HEADS * HEAD_DIM
    qkv_cols = qkv_weight.shape[1]
    out_cols = out_weight.shape[0]
    ff_cols = gate_weight.shape[1]
    ff_half = -(-ff_cols // 256) * 128
    flips = range(row_count)
    spans = REACH // row_count + 1
    window_rows = (REACH + 1) * block
    group_rows = HEADS // KV_HEADS * block
    spare = 16

    place = col_place * row_count + row_place
    first = place * block
    places = jnp.stack([row_place, first, col_place]).astype(jnp.int32)
    query_index = first + jnp.arange(block, dtype=jnp.int32)
    _, position = locate(query_index, seq_lens[0])
    cosine, sine = [jnp.concatenate([t, t], 1) for t in rope_tables(position)]
    start = (query_index - position)[:, None]

    both = exchange_row(
        call(
            pack_tokens_kernel,
            [((block + spare, 2 * part), bf16)] * 4,
            [places, hidden_in.T, out_grad.T, norm1_gain[None, :], norm2_gain[None, :]],
            [SMEM] + [VMEM] * 4,
            [pltpu.VMEM((quarter, 2 * part), bf16)],
        )
    )

    [packed] = call(
        pack_kernel,
        [((qkv_cols + out_cols, part + spare), bf16)],
        [qkv_weight.T, qkv_bias[:, None], out_weight],
    )

    def whole_cols(blocks, shapes, first=()):
        return call(
            assemble_kernel,
            [((col_count, *shape), bf16) for shape in shapes],
            [places, *blocks],
            [SMEM] + [VMEM] * 4,
            (),
            first,
        )

    upstream_low, upstream_send = call(
        join_upstream_kernel, [((block, width), bf16)] * 2, [*both]
    )
    qkv_block, out_block = whole_cols(
        gather_col(packed), [(qkv_cols, part + spare), (out_cols, part)], [upstream_low]
    )
    qkv_near = swap(qkv_block, "row", 1)
    qkv_far = swap(qkv_block, "row", 2)
    upstream_all = lax.all_gather(after(upstream_send, qkv_near), "col", axis=0)
    qkv_far = after(qkv_far, upstream_all)
    qkv_all = [qkv_block, qkv_near, qkv_far, swap(qkv_far, "row", 1)]

    out_come = swap(after(out_block, qkv_all[2]), "row", 2)

    inputs_low, queries, own_pair, gains, other_normed1 = call(
        project_kernel,
        [
            ((block, width), bf16),
            ((block, query_width), bf16),
            ((block, pair_width), bf16),
            ((2, width), f32),
            ((block, width // 2), bf16),
        ],
        [*both, *qkv_all, cosine, sine],
    )
    other_normed1 = swap(other_normed1, "row", 1)
    out_come = after(out_come, own_pair)
    out_blocks = [out_block, swap(out_block, "row", 1), out_come, swap(out_come, "row", 1)]

    [ff_packed] = call(
        pack_feed_kernel,
        [((3 * part, 2 * ff_half), bf16)],
        [gate_weight, up_weight, down_weight.T],
        None,
        (),
        [qkv_block],
    )

    from_cols = [own_pair] + [shifted(own_pair, "col", back) for back in range(1, spans)]
    from_cols = gather_row(jnp.concatenate(from_cols, 0))
    ff_packed = after(ff_packed, from_cols[2], out_blocks[2])
    ff_come = swap(ff_packed, "row", 2)
    attended, window, lse, middle, normed2 = call(
        attend_kernel,
        [
            ((block, query_width), bf16),
            ((window_rows, pair_width), bf16),
            ((KV_HEADS, group_rows, 1), f32),
            ((block, width), f32),
            ((block, width), bf16),
        ],
        [places, queries, *from_cols, start, inputs_low, *out_blocks, gains],
        [SMEM] + [VMEM] * 12,
        [
            pltpu.VMEM((row_count, spans, block, pair_width), bf16),
            pltpu.VMEM((group_rows, HEAD_DIM), bf16),
            pltpu.VMEM((group_rows, window_rows), f32),
        ],
    )
    other_attended = swap(attended, "row", 1)
    upstream_other = swap(upstream_all, "row", 1)
    normed2_all = lax.all_gather(normed2, "col", axis=0, tiled=True)
    normed2_other = swap(normed2_all, "row", 1)
    ff_come = after(ff_come, normed2_all)
    ff_blocks = [ff_packed, swap(ff_packed, "row", 1), ff_come, swap(ff_come, "row", 1)]

    grad_mine, grad_give, layer_mine, layer_give, ff_mine, ff_away = call(
        feed_kernel,
        [((quarter, width), bf16)] * 4 + [((3, 2 * part, ff_half), bf16)] * 2,
        [places, normed2_all, normed2_other, upstream_all, upstream_other, *ff_blocks],
        [SMEM] + [VMEM] * 4 + [ANY] * 4,
        [pltpu.VMEM((width, ff_half), bf16)] * 3
        + [pltpu.VMEM((2, quarter, width), bf16)] * 2
        + [pltpu.VMEM((2, width, quarter), bf16)] * 2
        + [pltpu.VMEM((2, quarter, ff_half), bf16)] * 3
        + [pltpu.VMEM((2, quarter, ff_half), f32), pltpu.SemaphoreType.DMA((3, 4))],
    )
    grad_normed2 = exchange_col(
        call(
            split_tokens_kernel,
            [((block, width), bf16)] * 4,
            [places, grad_mine, swap(grad_give, "row", 1)],
            [SMEM, VMEM, VMEM],
            [pltpu.VMEM((quarter, width), bf16)],
        )
    )

    def near_sum(near, own, first=()):
        return call(
            add_kernel,
            [(own.shape[1:], bf16)] * 2,
            [own, swap(near, "row", 1)],
            None,
            (),
            first,
        )

    layer_out = call(
        split_tokens_kernel,
        [((block, width), bf16)] * 4,
        [places, layer_mine, swap(layer_give, "row", 1)],
        [SMEM, VMEM, VMEM],
        [pltpu.VMEM((quarter, width), bf16)],
    )
    grad_middle, middle_low, gain2_sums, other_low = call(
        norm2_back_kernel,
        [
            ((block, width), f32),
            ((block, width), bf16),
            ((1, width), f32),
            ((block, width // 2), bf16),
        ],
        [*grad_normed2, middle, upstream_low, gains],
        None,
        (),
        [layer_out[0]],
    )
    layer_out = exchange_col(all_after(layer_out, middle_low))

    ff_kept, ff_give = call(
        feed_sum_kernel,
        [((3, part, ff_half), bf16)] * 2,
        [ff_mine, swap(ff_away, "row", 2)],
        None,
        (),
        [middle_low],
    )
    [ff_grad] = call(
        feed_join_kernel,
        [((3, part, ff_cols), bf16)],
        [places, ff_kept, swap(ff_give, "row", 1)],
        [SMEM, VMEM, VMEM],
        [pltpu.VMEM((3, part, 2 * ff_half), bf16)],
    )
    ff_come = over_groups_start(ff_grad)
    query_a, query_b, pair_near1, pair_near3, pair_own = call(
        attend_back_kernel,
        [((block, query_width // 2), bf16)] * 2
        + [((spans, block, pair_width), bf16)] * 2
        + [((2, spans, block, pair_width), bf16)],
        [places, queries, window, start, lse, middle_low, *out_blocks, cosine, sine],
        [SMEM] + [VMEM] * 11,
        [pltpu.VMEM((group_rows, HEAD_DIM), bf16)] * 2
        + [pltpu.VMEM((group_rows, window_rows), f32)] * 2
        + [pltpu.VMEM((group_rows, window_rows), bf16)] * 2
        + [pltpu.VMEM((block, query_width), f32), pltpu.VMEM((2, spans, block, pair_width), bf16)],
        [ff_kept],
    )
    held = (query_width // 32, 32, part + spare)
    partial1, query_mine, query_away = call(
        tail_query_kernel,
        [((block, width), f32)] + [((2 * held[0], *held[1:]), bf16)] * 2,
        [
            inputs_low,
            gains,
            query_a,
            query_b,
            other_normed1,
            swap(after(query_a, *layer_out[1:]), "row", 1),
            swap(query_b, "row", 1),
            middle_low,
            attended,
            swap(after(other_low, pair_own), "row", 1),
            other_attended,
            *qkv_all,
        ],
        None,
        (),
        [ff_grad],
    )

    pair_mine, pair_away = call(
        add_halves_kernel,
        [(pair_own.shape[1:], bf16)] * 2,
        [pair_own, swap(pair_near1, "row", 1), swap(pair_near3, "row", 1)],
        None,
        (),
        [query_mine],
    )
    pair_come = swap(pair_away, "row", 2)
    pair_sums = pair_mine.astype(f32) + pair_come.astype(f32)
    pair_back = [
        shifted(kept(pair_sums[back]), "col", -back)
        for back in range(1, spans)
    ]

    *results, pair_w_near, pair_w_own = call(
        tail_pair_kernel,
        [((3, block, part), bf16)] * 4 + [((2, pair_width // 32 + 1, 32, part + spare), bf16)] * 2,
        [
            inputs_low,
            gains,
            grad_middle,
            partial1,
            pair_sums[0],
            *pair_back,
            *qkv_all,
            gain2_sums,
            cosine,
            sine,
            middle,
            *layer_out,
        ],
        None,
        (),
        [query_away],
    )
    cut = qkv_cols // 32
    piece = (cut + held[0] // col_count, *held[1:])
    query_pieces = exchange_col(
        call(
            split_kernel,
            [(piece, bf16)] * 4,
            [places, query_mine, swap(query_away, "row", 2)],
            [SMEM, VMEM, VMEM],
            [pltpu.VMEM((4, *piece), bf16)],
            [pair_w_near, ff_come],
        )
    )
    pair_w_mine = scatter_far(*near_sum(pair_w_near, pair_w_own, [query_pieces[0]]))
    pair_low = kept(pair_w_mine)
    pair_w_grad = add_pieces(gather_col(pair_low))
    query_grad = add_pieces(query_pieces)
    results = exchange_row(all_after(results, kept(pair_w_grad)))
    results = jnp.concatenate(_in_order(results, row_place), 1)

    ff_grad = over_groups_end(ff_grad, ff_come)
    gate_grad, up_grad, down_grad = ff_grad[0], ff_grad[1], ff_grad[2]
    out_w_grad = over_groups(query_grad[cut:]).reshape(-1, part + spare)[:, :part]
    last = jnp.where(col_place == col_count - 1, 1.0, 0.0)
    pair_blocks = pair_width // 32
    qkv_grad = query_grad[:cut] + last * jnp.pad(
        pair_w_grad[:pair_blocks], ((cut - pair_blocks, 0), (0, 0), (0, 0))
    )
    qkv_grad = kept(jnp.concatenate([qkv_grad, pair_w_grad[pair_blocks:]], 0))
    qkv_grad = over_groups(qkv_grad)
    qkv_grad = qkv_grad.reshape(-1, part + spare)

    return (
        results[2],
        results[0].astype(f32) + results[1].astype(f32),
        qkv_grad[qkv_cols, :part],
        qkv_grad[:qkv_cols, :part].T,
        qkv_grad[:qkv_cols, part],
        out_w_grad,
        qkv_grad[qkv_cols + 1, :part],
        gate_grad,
        up_grad,
        down_grad.T,
    )


def _in_order(blocks, place):
    stacked = jnp.stack(blocks, 0)
    return [pick(stacked, place ^ k) for k in range(len(blocks))]


def solution(mesh):
    return jax.shard_map(
        body,
        mesh=mesh,
        in_specs=(
            P(("dp", "col"), "row"),
            P("row"),
            P("row", "col"),
            P("col"),
            P("col", "row"),
            P("row"),
            P("row", "col"),
            P("row", "col"),
            P("col", "row"),
            P("dp", None),
            P(("dp", "col"), "row"),
        ),
        out_specs=(
            P(("dp", "col"), "row"),
            P(("dp", "col"), "row"),
            P("row"),
            P("row", "col"),
            P("col"),
            P("col", "row"),
            P("row"),
            P("row", "col"),
            P("row", "col"),
            P("col", "row"),
        ),
        check_vma=False,
    )
```

```python
import jax
import jax.numpy as jnp
from jax import lax
from jax.experimental import pallas as pl
from jax.experimental.pallas import tpu as pltpu
from jax.sharding import PartitionSpec as P

HEADS = 14
KV_HEADS = 2
HEAD_DIM = 64
REACH = 8


norm_eps = 1e-06
rope_base = 1000000.0
masked_score = -1e30

bf16 = jnp.bfloat16
f32 = jnp.float32


def swap(array, axis, flip):
    count = lax.axis_size(axis)
    return lax.ppermute(array, axis, [(i, i ^ flip) for i in range(count)])


def shifted(array, axis, by):
    count = lax.axis_size(axis)
    pairs = [(i, i + by) for i in range(count) if 0 <= i + by < count]
    return lax.ppermute(array, axis, pairs)


def pick(array, index):
    return lax.dynamic_index_in_dim(array, index, 0, keepdims=False)


def after(array, *others):
    def kernel(*refs):
        pass

    whole = pl.BlockSpec(memory_space=pl.ANY)
    return pl.pallas_call(
        kernel,
        out_shape=jax.ShapeDtypeStruct(array.shape, array.dtype),
        in_specs=[whole] * (1 + len(others)),
        out_specs=whole,
        input_output_aliases={0: 0},
        cost_estimate=pl.CostEstimate(flops=0, bytes_accessed=0, transcendentals=0),
    )(array, *others)


def all_after(arrays, *others):
    count = len(arrays)

    def kernel(*refs):
        pass

    whole = pl.BlockSpec(memory_space=pl.ANY)
    return pl.pallas_call(
        kernel,
        out_shape=[jax.ShapeDtypeStruct(a.shape, a.dtype) for a in arrays],
        in_specs=[whole] * (count + len(others)),
        out_specs=[whole] * count,
        input_output_aliases={k: k for k in range(count)},
        cost_estimate=pl.CostEstimate(flops=0, bytes_accessed=0, transcendentals=0),
    )(*arrays, *others)


def kept(values):
    return lax.optimization_barrier(values.astype(bf16))


def gather_col(block):
    far, next_far, near = [swap(block, "col", k) for k in (3, 2, 1)]
    return [block, near, next_far, far]


def gather_row(block):
    other = swap(block, "row", 2)
    return [block, swap(block, "row", 1), other, swap(other, "row", 1)]


def exchange_col(blocks):
    far, next_far, near = [swap(blocks[k], "col", k) for k in (3, 2, 1)]
    return [blocks[0], near, next_far, far]


def add_pieces(pieces):
    a, b, c, d = [p.astype(f32) for p in pieces]
    return (a + b) + (c + d)


def scatter_far(mine, away):
    return mine.astype(f32) + swap(away, "row", 2).astype(f32)


def over_groups_start(low):
    if lax.axis_size("dp") == 2:
        return swap(low, "dp", 1)
    return lax.psum(low, "dp")


def over_groups_end(low, come):
    if lax.axis_size("dp") == 2:
        return low.astype(f32) + come.astype(f32)
    return come.astype(f32)


def over_groups(values):
    low = kept(values)
    return over_groups_end(low, over_groups_start(low))


def exchange_row(blocks):
    return [blocks[0]] + [swap(blocks[k], "row", k) for k in (1, 2, 3)]


def locate(indices, lengths):
    ends = jnp.cumsum(lengths)
    starts = ends - lengths
    segment = jnp.sum((indices[:, None] >= ends[None, :]).astype(jnp.int32), 1)
    chosen = segment[:, None] == jnp.arange(lengths.shape[0], dtype=jnp.int32)[None, :]
    position = indices - jnp.sum(jnp.where(chosen, starts[None, :], 0), 1)
    return (segment, position)


def rope_tables(position):
    half = HEAD_DIM // 2
    rates = rope_base ** (-(jnp.arange(half, dtype=f32) * 2.0) / HEAD_DIM)
    angles = position.astype(f32)[:, None] * rates[None, :]
    cosine = jnp.cos(angles)
    sine = jnp.sin(angles)
    return (jnp.concatenate([cosine, cosine], -1), jnp.concatenate([sine, sine], -1))


def lane_half(shape):
    return lax.broadcasted_iota(jnp.int32, shape, 1) % HEAD_DIM < HEAD_DIM // 2


def lane_roll(values, by):
    by = by % values.shape[1]
    return jnp.concatenate([values[:, -by:], values[:, :-by]], 1)


def turned(values):
    half = HEAD_DIM // 2
    return jnp.where(lane_half(values.shape), -lane_roll(values, -half), lane_roll(values, half))


def turned_back(values):
    half = HEAD_DIM // 2
    return jnp.where(lane_half(values.shape), lane_roll(values, -half), -lane_roll(values, half))


def tiled(table, width):
    return jnp.concatenate([table] * (width // table.shape[1]), 1)


def dot_nt(left, right):
    return lax.dot_general(left, right, (((1,), (1,)), ((), ())), preferred_element_type=f32)


def dot_tn(left, right):
    return lax.dot_general(left, right, (((0,), (0,)), ((), ())), preferred_element_type=f32)


def dot_nn(left, right):
    return jnp.dot(left, right, preferred_element_type=f32)


def flat(ref):
    return ref[...].reshape(-1, ref.shape[-1])


def hop_slot(hop, row_place, row_count):
    their_row = (row_place - hop + 2 * REACH * row_count) % row_count
    return row_place ^ their_row, (hop + their_row - row_place) // row_count


def attend_kernel(
    place_ref, queries_ref, from0, from1, from2, from3, start_ref, inputs_ref, out0, out1, out2, out3, gain_ref, attended_ref, window_ref, lse_ref, middle_ref, normed_ref, held, stack, scores,
):
    block = queries_ref.shape[0]
    spans = from0.shape[0] // block
    heads = HEADS // KV_HEADS
    rows = heads * block
    row_place, first = place_ref[0], place_ref[1]
    for flip, ref in enumerate((from0, from1, from2, from3)):
        for back in range(spans):
            held[flip, back] = ref[back * block : (back + 1) * block, :]
    for at in range(REACH + 1):
        flip, back = hop_slot(REACH - at, row_place, 4)
        window_ref[at * block : (at + 1) * block, :] = held[flip, back]
    keys_in = (REACH + 1) * block
    key_index = first - REACH * block + lax.broadcasted_iota(jnp.int32, (block, keys_in), 1)
    query_index = first + lax.broadcasted_iota(jnp.int32, (block, keys_in), 0)
    allowed = (key_index >= start_ref[...]) & (key_index <= query_index)
    bias = jnp.where(allowed, 0.0, masked_score)
    for group in range(KV_HEADS):
        for h in range(heads):
            at = (group * heads + h) * HEAD_DIM
            stack[h * block : (h + 1) * block, :] = queries_ref[:, at : at + HEAD_DIM] * 0.125
        keys = window_ref[:, group * HEAD_DIM : (group + 1) * HEAD_DIM]
        values = window_ref[:, (KV_HEADS + group) * HEAD_DIM : (KV_HEADS + group + 1) * HEAD_DIM]
        scores[...] = dot_nt(stack[...], keys)
        for h in range(heads):
            at = (group * heads + h) * HEAD_DIM
            mine = scores[h * block : (h + 1) * block, :] + bias
            top = jnp.max(mine, 1, keepdims=True)
            raised = jnp.exp(mine - top)
            total = jnp.sum(raised, 1, keepdims=True)
            weights = (raised * (1.0 / total)).astype(bf16)
            attended_ref[:, at : at + HEAD_DIM] = dot_nn(weights, values).astype(bf16)
            lse_ref[group, h * block : (h + 1) * block, :] = top + jnp.log(total)
    attended = attended_ref[...]
    projected = jnp.concatenate(
        [dot_nn(attended, flat(w)) for w in (out0, out1, out2, out3)], 1
    )
    middle = inputs_ref[...].astype(f32) + projected
    middle_ref[...] = middle
    inv = lax.rsqrt(jnp.mean(middle * middle, 1, keepdims=True) + norm_eps)
    normed_ref[...] = (middle * inv * gain_ref[1:2, :]).astype(bf16)


def attend_back_kernel(
    place_ref, queries_ref, window_ref, start_ref, lse_ref, middle_low_ref, out0, out1, out2, out3, cos_ref, sin_ref,
    query_a_ref, query_b_ref, near1_ref, near3_ref, own_ref, stack, outer, scores, probs_grad, low_scores, low_probs, heads_out, near_ref,
):
    block = queries_ref.shape[0]
    part = out0.shape[-1]
    heads = HEADS // KV_HEADS
    rows = heads * block
    row_place, first = place_ref[0], place_ref[1]
    keys_in = (REACH + 1) * block
    key_index = first - REACH * block + lax.broadcasted_iota(jnp.int32, (block, keys_in), 1)
    query_index = first + lax.broadcasted_iota(jnp.int32, (block, keys_in), 0)
    allowed = (key_index >= start_ref[...]) & (key_index <= query_index)
    bias = jnp.where(allowed, 0.0, masked_score)
    grads = dot_nt(middle_low_ref[:, :part], flat(out0))
    for k, w in ((1, out1), (2, out2), (3, out3)):
        grads += dot_nt(middle_low_ref[:, k * part : (k + 1) * part], flat(w))
    grads = grads.astype(bf16)
    near_ref[...] = jnp.zeros(near_ref.shape, bf16)
    own_ref[...] = jnp.zeros(own_ref.shape, bf16)
    for group in range(KV_HEADS):
        for h in range(heads):
            at = (group * heads + h) * HEAD_DIM
            stack[h * block : (h + 1) * block, :] = queries_ref[:, at : at + HEAD_DIM] * 0.125
            outer[h * block : (h + 1) * block, :] = grads[:, at : at + HEAD_DIM]
        keys = window_ref[:, group * HEAD_DIM : (group + 1) * HEAD_DIM]
        values = window_ref[:, (KV_HEADS + group) * HEAD_DIM : (KV_HEADS + group + 1) * HEAD_DIM]
        scores[...] = dot_nt(stack[...], keys)
        probs_grad[...] = dot_nt(outer[...], values)
        for h in range(heads):
            here = slice(h * block, (h + 1) * block)
            probs = jnp.exp(scores[here, :] + bias - lse_ref[group, here, :])
            moved = probs * probs_grad[here, :]
            total = jnp.sum(moved, 1, keepdims=True)
            low_scores[here, :] = (moved - probs * total).astype(bf16)
            low_probs[here, :] = probs.astype(bf16)
        query_grads = dot_nn(low_scores[...], keys) * 0.125
        for h in range(heads):
            at = (group * heads + h) * HEAD_DIM
            heads_out[:, at : at + HEAD_DIM] = query_grads[h * block : (h + 1) * block, :]
        key_grads = dot_tn(stack[...], low_scores[...]).T.astype(bf16)
        value_grads = dot_tn(outer[...], low_probs[...]).T.astype(bf16)
        for at in range(REACH + 1):
            flip, back = hop_slot(REACH - at, row_place, 4)
            here = slice(at * block, (at + 1) * block)
            key_lanes = slice(group * HEAD_DIM, (group + 1) * HEAD_DIM)
            value_lanes = slice((KV_HEADS + group) * HEAD_DIM, (KV_HEADS + group + 1) * HEAD_DIM)

            @pl.when(flip % 2 == 1)
            def _():
                near_ref[flip // 2, back, :, key_lanes] = key_grads[here, :]
                near_ref[flip // 2, back, :, value_lanes] = value_grads[here, :]

            @pl.when(flip % 2 == 0)
            def _():
                own_ref[flip // 2, back, :, key_lanes] = key_grads[here, :]
                own_ref[flip // 2, back, :, value_lanes] = value_grads[here, :]

    near1_ref[...] = near_ref[0]
    near3_ref[...] = near_ref[1]
    whole = heads_out[...]
    cosine, sine = tiled(cos_ref[...], whole.shape[1]), tiled(sin_ref[...], whole.shape[1])
    whole = (whole * cosine + turned_back(whole * sine)).astype(bf16)
    half = query_a_ref.shape[1]
    query_a_ref[...] = whole[:, :half]
    query_b_ref[...] = whole[:, half:]


def other_core(values):
    part = values.shape[1] // 4
    return jnp.concatenate([values[:, part : 2 * part], values[:, 3 * part :]], 1)


def pack_tokens_kernel(place_ref, inputs_ref, upstream_ref, gain1_ref, gain2_ref, *refs):
    outs, tokens = refs[:4], refs[4]
    part, count = inputs_ref.shape
    block = count // 4
    tokens[:, :part] = inputs_ref[...].astype(f32).T.astype(bf16)
    tokens[:, part:] = upstream_ref[...].astype(f32).T.astype(bf16)
    spare = outs[0].shape[0] - block
    rows = []
    for ref in (gain1_ref, gain2_ref):
        rest = ref[...]
        for _ in range(3):
            high = rest.astype(bf16).astype(f32)
            rows.append(high)
            rest = rest - high
    rows.append(jnp.zeros((spare - len(rows), part), f32))
    rows = jnp.concatenate(rows, 0)
    rows = jnp.concatenate([rows, jnp.zeros(rows.shape, f32)], 1).astype(bf16)
    for k, out in enumerate(outs):
        start = pl.multiple_of((place_ref[0] ^ k) * block, 16)
        out[:block, :] = tokens[pl.ds(start, block), :]
        out[block:, :] = rows


def pack_kernel(qkv_ref, bias_ref, out_ref, packed_ref):
    cols, part = qkv_ref.shape
    spare = packed_ref.shape[1] - part
    first = lax.broadcasted_iota(jnp.int32, (cols, spare), 1) == 0
    bias = jnp.where(first, bias_ref[...].astype(f32), 0.0).astype(bf16)
    packed_ref[:cols, :] = jnp.concatenate([qkv_ref[...], bias], 1)
    rows = out_ref.shape[0]
    packed_ref[cols:, :] = jnp.concatenate([out_ref[...], jnp.zeros((rows, spare), bf16)], 1)


def assemble_kernel(place_ref, *refs):
    blocks, outs = refs[:4], refs[4:]
    for j in range(4):
        start = 0
        for out in outs:
            out[place_ref[2] ^ j] = blocks[j][start : start + out.shape[1], : out.shape[2]]
            start += out.shape[1]


def join_upstream_kernel(*refs):
    both, out_ref, again_ref = refs[:4], refs[4], refs[5]
    block = out_ref.shape[0]
    part = both[0].shape[1] // 2
    whole = jnp.concatenate([b[:block, part:] for b in both], 1)
    out_ref[...] = whole
    again_ref[...] = whole


def pack_feed_kernel(gate_ref, up_ref, down_ref, packed_ref):
    part, cols = gate_ref.shape
    for at, ref in enumerate((gate_ref, up_ref, down_ref)):
        packed_ref[at * part : (at + 1) * part, :cols] = ref[...]
    packed_ref[:, cols:] = jnp.zeros((3 * part, packed_ref.shape[1] - cols), bf16)


def add_kernel(own_ref, come_ref, mine_ref, away_ref):
    mine_ref[...] = (own_ref[0].astype(f32) + come_ref[0].astype(f32)).astype(bf16)
    away_ref[...] = (own_ref[1].astype(f32) + come_ref[1].astype(f32)).astype(bf16)


def add_halves_kernel(own_ref, first_ref, second_ref, mine_ref, away_ref):
    mine_ref[...] = (own_ref[0].astype(f32) + first_ref[...].astype(f32)).astype(bf16)
    away_ref[...] = (own_ref[1].astype(f32) + second_ref[...].astype(f32)).astype(bf16)


def project_kernel(*refs):
    both, weights = refs[:4], refs[4:8]
    cos_ref, sin_ref = refs[8:10]
    inputs_ref, queries_ref, pair_ref, gains_ref, other_ref = refs[10:]
    part = both[0].shape[1] // 2
    block = inputs_ref.shape[0]
    spare = weights[0].shape[-1] - part
    inputs_low = jnp.concatenate([b[:block, :part] for b in both], 1)
    inputs_ref[...] = inputs_low
    gains = [b[block : block + 16, :part].astype(f32) for b in both]
    for to in range(2):
        at = 3 * to
        gains_ref[to : to + 1, :] = jnp.concatenate(
            [g[at : at + 1] + g[at + 1 : at + 2] + g[at + 2 : at + 3] for g in gains], 1
        )
    inputs = inputs_low.astype(f32)
    inv = lax.rsqrt(jnp.mean(inputs * inputs, 1, keepdims=True) + norm_eps)
    normed = (inputs * inv * gains_ref[0:1, :]).astype(bf16)
    other_ref[...] = other_core(normed)
    one = (lax.broadcasted_iota(jnp.int32, (block, spare), 1) == 0).astype(f32).astype(bf16)
    projected = dot_nt(jnp.concatenate([normed[:, :part], one], 1), flat(weights[0]))
    for k in range(1, 4):
        mine = normed[:, k * part : (k + 1) * part]
        projected = projected + dot_nt(
            jnp.concatenate([mine, jnp.zeros_like(one)], 1), flat(weights[k])
        )
    turning = (HEADS + KV_HEADS) * HEAD_DIM
    whole = projected[:, :turning]
    cosine, sine = tiled(cos_ref[...], turning), tiled(sin_ref[...], turning)
    whole = (whole * cosine + turned(whole) * sine).astype(bf16)
    queries_ref[...] = whole[:, : HEADS * HEAD_DIM]
    pair_ref[...] = jnp.concatenate(
        [whole[:, HEADS * HEAD_DIM :], projected[:, turning:].astype(bf16)], 1
    )


def load_blocks(packed, at, row_place, into, sems):
    part, cols = into.shape[0] // 4, into.shape[1]
    lanes = pl.ds(pl.multiple_of((row_place % 2) * cols, 128), cols)
    copies = []
    for k in range(4):
        copies.append(
            pltpu.make_async_copy(
                packed[k].at[pl.ds(at * part, part), lanes],
                into.at[pl.ds(k * part, part)],
                sems.at[k],
            )
        )
    for copy in copies:
        copy.start()
    return copies


def other_order(values):
    part = values.shape[1] // 4
    blocks = [values[:, k * part : (k + 1) * part] for k in (1, 0, 3, 2)]
    return jnp.concatenate(blocks, 1)


def feed_kernel(place_ref, normed_ref, normed_other_ref, *refs):
    upstreams, packed, refs = refs[:2], refs[2:6], refs[6:]
    grad_outs, layer_outs, mine_ref, away_ref = refs[:2], refs[2:4], refs[4], refs[5]
    gate_w, up_w, down_w = refs[6:9]
    normed, upstream, normed_t, upstream_t = refs[9:13]
    hidden, gate_grad, up_grad, grad_hidden, sems = refs[13:]
    row_place = place_ref[0]
    down_copies = load_blocks(packed, 2, row_place, down_w, sems.at[0])
    gate_copies = load_blocks(packed, 0, row_place, gate_w, sems.at[1])
    up_copies = load_blocks(packed, 1, row_place, up_w, sems.at[2])
    for at, n_ref in enumerate((normed_ref, normed_other_ref)):
        values = flat(upstreams[at])
        upstream[at] = other_order(values) if at else values
        values = n_ref[...]
        normed[at] = other_order(values) if at else values
        for ref, into_t in ((normed, normed_t), (upstream, upstream_t)):
            into_t[at] = ref[at].astype(f32).T.astype(bf16)
    cols = hidden.shape[2]
    cuts = [slice(lo, min(lo + 384, cols)) for lo in range(0, cols, 384)]
    for copy in down_copies:
        copy.wait()
    for at in range(2):
        for cut in cuts:
            grad_hidden[at, :, cut] = dot_nn(upstream[at], down_w[:, cut])
    for copy in gate_copies + up_copies:
        copy.wait()
    for at in range(2):
        for cut in cuts:
            gate = dot_nn(normed[at], gate_w[:, cut])
            up = dot_nn(normed[at], up_w[:, cut])
            sigma = 1.0 / (1.0 + jnp.exp(-gate))
            silu = gate * sigma
            grad = grad_hidden[at, :, cut]
            hidden[at, :, cut] = (silu * up).astype(bf16)
            gate_grad[at, :, cut] = (
                grad * up * sigma * (1.0 + gate * (1.0 - sigma))
            ).astype(bf16)
            up_grad[at, :, cut] = (grad * silu).astype(bf16)
    for at in range(2):
        total = dot_nt(gate_grad[at], gate_w[...]) + dot_nt(up_grad[at], up_w[...])
        total = total.astype(bf16)
        grad_outs[at][...] = other_order(total) if at else total
        total = dot_nt(hidden[at], down_w[...]).astype(bf16)
        layer_outs[at][...] = other_order(total) if at else total
    part = gate_w.shape[0] // 4
    for to, (left, right) in enumerate(
        ((normed_t, gate_grad), (normed_t, up_grad), (upstream_t, hidden))
    ):
        for cut in cuts:
            whole = dot_nn(left[0], right[0, :, cut]) + dot_nn(left[1], right[1, :, cut])
            whole = whole.astype(bf16)
            mine_ref[to, :, cut] = whole[: 2 * part]
            away_ref[to, :, cut] = whole[2 * part :]


def split_tokens_kernel(place_ref, mine_ref, come_ref, *outs):
    total, outs = outs[-1], outs[:-1]
    total[...] = (mine_ref[...].astype(f32) + come_ref[...].astype(f32)).astype(bf16)
    block = outs[0].shape[0]
    for k in range(4):
        start = pl.multiple_of((place_ref[2] ^ k) * block, 16)
        outs[k][...] = total[pl.ds(start, block), :]


def feed_sum_kernel(mine_ref, come_ref, kept_ref, give_ref):
    part = kept_ref.shape[1]
    total = (mine_ref[...].astype(f32) + come_ref[...].astype(f32)).astype(bf16)
    kept_ref[...] = total[:, :part]
    give_ref[...] = total[:, part:]


def feed_join_kernel(place_ref, mine_ref, come_ref, out_ref, whole):
    cols = mine_ref.shape[2]
    core = place_ref[0] % 2
    whole[:, :, pl.ds(pl.multiple_of(core * cols, 128), cols)] = mine_ref[...]
    whole[:, :, pl.ds(pl.multiple_of((1 - core) * cols, 128), cols)] = come_ref[...]
    out_ref[...] = whole[:, :, : out_ref.shape[2]]


def norm2_back_kernel(*refs):
    pieces, middle_ref, upstream_ref, gains_ref = refs[:4], refs[4], refs[5], refs[6]
    grad_ref, low_ref, sums_ref, other_ref = refs[-4:]
    grad = (pieces[0][...].astype(f32) + pieces[1][...].astype(f32)) + (
        pieces[2][...].astype(f32) + pieces[3][...].astype(f32)
    )
    middle = middle_ref[...]
    width = middle.shape[1]
    inv = lax.rsqrt(jnp.mean(middle * middle, 1, keepdims=True) + norm_eps)
    sums_ref[...] = jnp.sum(grad * middle * inv, 0, keepdims=True)
    scaled = grad * gains_ref[1:2, :]
    along = jnp.sum(scaled * middle, 1, keepdims=True)
    out = upstream_ref[: middle.shape[0], :].astype(f32) + inv * scaled - middle * (inv * inv * inv * along / width)
    grad_ref[...] = out
    low_ref[...] = out.astype(bf16)
    other_ref[...] = other_core(out).astype(bf16)


def store_weight_grad(near_ref, own_ref, at, grads, normed):
    part = normed.shape[1] // 4
    spare = near_ref.shape[-1] - part
    ones = jnp.ones((grads.shape[0], spare), f32).astype(bf16)
    blocks = grads.shape[1] // 32
    for ref, places in ((near_ref, (1, 3)), (own_ref, (0, 2))):
        for to, k in enumerate(places):
            mine = jnp.concatenate([normed[:, k * part : (k + 1) * part], ones], 1)
            whole = dot_tn(grads, mine).astype(bf16)
            ref[to, at : at + blocks] = whole.reshape(blocks, 32, part + spare)


def core_weight_grad(grads, normed, other_grads, other_normed, mine_ref, away_ref):
    part = normed.shape[1] // 4
    spare = mine_ref.shape[-1] - part
    both = jnp.concatenate([grads, other_grads], 0)
    ones = jnp.ones((both.shape[0], spare), f32).astype(bf16)
    for ref, k, at in ((mine_ref, 0, 0), (away_ref, 2, 1)):
        mine = normed[:, k * part : (k + 1) * part]
        other = other_normed[:, at * part : (at + 1) * part]
        mine = jnp.concatenate([jnp.concatenate([mine, other], 0), ones], 1)
        ref[...] = dot_tn(both, mine).astype(bf16).reshape(ref.shape)


def tail_query_kernel(*refs):
    inputs_ref, gains_ref, query_a, query_b, other_normed_ref, other_a, other_b = refs[:7]
    low_ref, attended_ref, other_low_ref, other_attended_ref = refs[7:11]
    weights = refs[11:15]
    partial_ref, mine_ref, away_ref = refs[15:]
    part = inputs_ref.shape[1] // 4
    grads = jnp.concatenate([query_a[...], query_b[...]], 1)
    other_grads = jnp.concatenate([other_a[...], other_b[...]], 1)
    cols = grads.shape[1]
    for k in range(4):
        partial_ref[:, k * part : (k + 1) * part] = dot_nn(grads, flat(weights[k])[:cols, :part])
    inputs = inputs_ref[...].astype(f32)
    inv = lax.rsqrt(jnp.mean(inputs * inputs, 1, keepdims=True) + norm_eps)
    normed = (inputs * inv * gains_ref[0:1, :]).astype(bf16)
    half = mine_ref.shape[0] // 2
    for at, (one, two, three, four) in enumerate(
        (
            (grads, normed, other_grads, other_normed_ref[...]),
            (attended_ref[...], low_ref[...], other_attended_ref[...], other_low_ref[...]),
        )
    ):
        here = pl.ds(at * half, half)
        core_weight_grad(one, two, three, four, mine_ref.at[here], away_ref.at[here])


def tail_pair_kernel(*refs):
    inputs_ref, gains_ref, middle_grad_ref, partial_ref = refs[:4]
    pair_refs, weights = refs[4:7], refs[7:11]
    sums2_ref, cos_ref, sin_ref, middle_ref = refs[11:15]
    layer_refs = refs[15:19]
    results = refs[19:23]
    near_ref, own_ref = refs[23:]
    block, width = inputs_ref.shape
    part = width // 4
    turning = KV_HEADS * HEAD_DIM
    pair = pair_refs[0][...] + pair_refs[1][...].astype(f32) + pair_refs[2][...].astype(f32)
    keys = pair[:, :turning]
    cosine, sine = tiled(cos_ref[...], turning), tiled(sin_ref[...], turning)
    keys = keys * cosine + turned_back(keys * sine)
    grads = jnp.concatenate([keys.astype(bf16), pair[:, turning:].astype(bf16)], 1)
    pair_cols = grads.shape[1]
    grad_normed = [dot_nn(grads, flat(w)[-pair_cols:, :part]) for w in weights]
    grad = partial_ref[...] + jnp.concatenate(grad_normed, 1)
    inputs = inputs_ref[...].astype(f32)
    gain = gains_ref[0:1, :]
    inv = lax.rsqrt(jnp.mean(inputs * inputs, 1, keepdims=True) + norm_eps)
    normed = (inputs * inv * gain).astype(bf16)
    sums1 = jnp.sum(grad * inputs * inv, 0, keepdims=True)
    scaled = grad * gain
    along = jnp.sum(scaled * inputs, 1, keepdims=True)
    out = middle_grad_ref[...] + inv * scaled - inputs * (inv * inv * inv * along / width)
    layer = (layer_refs[0][...].astype(f32) + layer_refs[1][...].astype(f32)) + (
        layer_refs[2][...].astype(f32) + layer_refs[3][...].astype(f32)
    )
    for at, values in enumerate((out.astype(bf16), (middle_ref[...] + layer).astype(bf16))):
        for k in range(4):
            results[k][at] = values[:, k * part : (k + 1) * part]
    store_weight_grad(near_ref, own_ref, 0, grads, normed)
    spare = near_ref.shape[-1] - part
    for ref, places in ((near_ref, (1, 3)), (own_ref, (0, 2))):
        for to, k in enumerate(places):
            here = slice(k * part, (k + 1) * part)
            lines = [sums1[:, here], sums2_ref[:, here], jnp.zeros((30, part), f32)]
            lines = jnp.concatenate(lines, 0)
            lines = jnp.concatenate([lines, jnp.zeros((32, spare), f32)], 1)
            ref[to, pair_cols // 32] = lines.astype(bf16)


def split_kernel(place_ref, mine_ref, come_ref, *refs):
    outs, pieces = refs[:4], refs[4]
    total = (mine_ref[...].astype(f32) + come_ref[...].astype(f32)).astype(bf16)
    count = outs[0].shape[0]
    half = total.shape[0] // 2
    upper, lower = count - half // 4, half // 4
    for c in range(4):
        piece = total[c * upper : min((c + 1) * upper, half)]
        held = piece.shape[0]
        pieces[c, :held] = piece
        if held < upper:
            pieces[c, held:upper] = jnp.zeros((upper - held, *total.shape[1:]), bf16)
        pieces[c, upper:] = total[half + c * lower : half + (c + 1) * lower]
    for j in range(4):
        outs[j][...] = pieces[place_ref[2] ^ j]


VMEM = pl.BlockSpec(memory_space=pltpu.VMEM)
SMEM = pl.BlockSpec(memory_space=pltpu.SMEM)
ANY = pl.BlockSpec(memory_space=pl.ANY)


def call(kernel, outs, operands, specs=None, scratch=(), first=()):
    seen = len(operands)
    specs = list(specs) if specs else [VMEM] * seen

    def run(*refs):
        kernel(*refs[:seen], *refs[seen + len(first) :])

    return pl.pallas_call(
        run,
        out_shape=[jax.ShapeDtypeStruct(shape, dtype) for shape, dtype in outs],
        in_specs=specs + [ANY] * len(first),
        out_specs=[VMEM] * len(outs),
        scratch_shapes=list(scratch),
        cost_estimate=pl.CostEstimate(flops=0, bytes_accessed=0, transcendentals=0),
        compiler_params=pltpu.CompilerParams(vmem_limit_bytes=56 * 2**20),
    )(*operands, *first)


def body(
    hidden_in,
    norm1_gain,
    qkv_weight,
    qkv_bias,
    out_weight,
    norm2_gain,
    gate_weight,
    up_weight,
    down_weight,
    seq_lens,
    out_grad,
):
    row_count = lax.axis_size("row")
    col_count = lax.axis_size("col")
    row_place = lax.axis_index("row")
    col_place = lax.axis_index("col")
    quarter, part = hidden_in.shape
    block = quarter // row_count
    width = part * row_count
    query_width = HEADS * HEAD_DIM
    pair_width = 2 * KV_HEADS * HEAD_DIM
    qkv_cols = qkv_weight.shape[1]
    out_cols = out_weight.shape[0]
    ff_cols = gate_weight.shape[1]
    ff_half = -(-ff_cols // 256) * 128
    flips = range(row_count)
    spans = REACH // row_count + 1
    window_rows = (REACH + 1) * block
    group_rows = HEADS // KV_HEADS * block
    spare = 16

    place = col_place * row_count + row_place
    first = place * block
    places = jnp.stack([row_place, first, col_place]).astype(jnp.int32)
    query_index = first + jnp.arange(block, dtype=jnp.int32)
    _, position = locate(query_index, seq_lens[0])
    cosine, sine = [jnp.concatenate([t, t], 1) for t in rope_tables(position)]
    start = (query_index - position)[:, None]

    both = exchange_row(
        call(
            pack_tokens_kernel,
            [((block + spare, 2 * part), bf16)] * 4,
            [places, hidden_in.T, out_grad.T, norm1_gain[None, :], norm2_gain[None, :]],
            [SMEM] + [VMEM] * 4,
            [pltpu.VMEM((quarter, 2 * part), bf16)],
        )
    )

    [packed] = call(
        pack_kernel,
        [((qkv_cols + out_cols, part + spare), bf16)],
        [qkv_weight.T, qkv_bias[:, None], out_weight],
    )

    def whole_cols(blocks, shapes, first=()):
        return call(
            assemble_kernel,
            [((col_count, *shape), bf16) for shape in shapes],
            [places, *blocks],
            [SMEM] + [VMEM] * 4,
            (),
            first,
        )

    upstream_low, upstream_send = call(
        join_upstream_kernel, [((block, width), bf16)] * 2, [*both]
    )
    qkv_block, out_block = whole_cols(
        gather_col(packed), [(qkv_cols, part + spare), (out_cols, part)], [upstream_low]
    )
    qkv_near = swap(qkv_block, "row", 1)
    qkv_far = swap(qkv_block, "row", 2)
    upstream_all = lax.all_gather(after(upstream_send, qkv_near), "col", axis=0)
    qkv_far = after(qkv_far, upstream_all)
    qkv_all = [qkv_block, qkv_near, qkv_far, swap(qkv_far, "row", 1)]

    out_come = swap(after(out_block, qkv_all[2]), "row", 2)

    inputs_low, queries, own_pair, gains, other_normed1 = call(
        project_kernel,
        [
            ((block, width), bf16),
            ((block, query_width), bf16),
            ((block, pair_width), bf16),
            ((2, width), f32),
            ((block, width // 2), bf16),
        ],
        [*both, *qkv_all, cosine, sine],
    )
    other_normed1 = swap(other_normed1, "row", 1)
    out_come = after(out_come, own_pair)
    out_blocks = [out_block, swap(out_block, "row", 1), out_come, swap(out_come, "row", 1)]

    [ff_packed] = call(
        pack_feed_kernel,
        [((3 * part, 2 * ff_half), bf16)],
        [gate_weight, up_weight, down_weight.T],
        None,
        (),
        [qkv_block],
    )

    from_cols = [own_pair] + [shifted(own_pair, "col", back) for back in range(1, spans)]
    from_cols = gather_row(jnp.concatenate(from_cols, 0))
    ff_packed = after(ff_packed, from_cols[2], out_blocks[2])
    ff_come = swap(ff_packed, "row", 2)
    attended, window, lse, middle, normed2 = call(
        attend_kernel,
        [
            ((block, query_width), bf16),
            ((window_rows, pair_width), bf16),
            ((KV_HEADS, group_rows, 1), f32),
            ((block, width), f32),
            ((block, width), bf16),
        ],
        [places, queries, *from_cols, start, inputs_low, *out_blocks, gains],
        [SMEM] + [VMEM] * 12,
        [
            pltpu.VMEM((row_count, spans, block, pair_width), bf16),
            pltpu.VMEM((group_rows, HEAD_DIM), bf16),
            pltpu.VMEM((group_rows, window_rows), f32),
        ],
    )
    other_attended = swap(attended, "row", 1)
    upstream_other = swap(upstream_all, "row", 1)
    normed2_all = lax.all_gather(normed2, "col", axis=0, tiled=True)
    normed2_other = swap(normed2_all, "row", 1)
    ff_come = after(ff_come, normed2_all)
    ff_blocks = [ff_packed, swap(ff_packed, "row", 1), ff_come, swap(ff_come, "row", 1)]

    grad_mine, grad_give, layer_mine, layer_give, ff_mine, ff_away = call(
        feed_kernel,
        [((quarter, width), bf16)] * 4 + [((3, 2 * part, ff_half), bf16)] * 2,
        [places, normed2_all, normed2_other, upstream_all, upstream_other, *ff_blocks],
        [SMEM] + [VMEM] * 4 + [ANY] * 4,
        [pltpu.VMEM((width, ff_half), bf16)] * 3
        + [pltpu.VMEM((2, quarter, width), bf16)] * 2
        + [pltpu.VMEM((2, width, quarter), bf16)] * 2
        + [pltpu.VMEM((2, quarter, ff_half), bf16)] * 3
        + [pltpu.VMEM((2, quarter, ff_half), f32), pltpu.SemaphoreType.DMA((3, 4))],
    )
    grad_normed2 = exchange_col(
        call(
            split_tokens_kernel,
            [((block, width), bf16)] * 4,
            [places, grad_mine, swap(grad_give, "row", 1)],
            [SMEM, VMEM, VMEM],
            [pltpu.VMEM((quarter, width), bf16)],
        )
    )

    def near_sum(near, own, first=()):
        return call(
            add_kernel,
            [(own.shape[1:], bf16)] * 2,
            [own, swap(near, "row", 1)],
            None,
            (),
            first,
        )

    layer_out = call(
        split_tokens_kernel,
        [((block, width), bf16)] * 4,
        [places, layer_mine, swap(layer_give, "row", 1)],
        [SMEM, VMEM, VMEM],
        [pltpu.VMEM((quarter, width), bf16)],
    )
    grad_middle, middle_low, gain2_sums, other_low = call(
        norm2_back_kernel,
        [
            ((block, width), f32),
            ((block, width), bf16),
            ((1, width), f32),
            ((block, width // 2), bf16),
        ],
        [*grad_normed2, middle, upstream_low, gains],
        None,
        (),
        [layer_out[0]],
    )
    layer_out = exchange_col(all_after(layer_out, middle_low))

    ff_kept, ff_give = call(
        feed_sum_kernel,
        [((3, part, ff_half), bf16)] * 2,
        [ff_mine, swap(ff_away, "row", 2)],
        None,
        (),
        [middle_low],
    )
    query_a, query_b, pair_near1, pair_near3, pair_own = call(
        attend_back_kernel,
        [((block, query_width // 2), bf16)] * 2
        + [((spans, block, pair_width), bf16)] * 2
        + [((2, spans, block, pair_width), bf16)],
        [places, queries, window, start, lse, middle_low, *out_blocks, cosine, sine],
        [SMEM] + [VMEM] * 11,
        [pltpu.VMEM((group_rows, HEAD_DIM), bf16)] * 2
        + [pltpu.VMEM((group_rows, window_rows), f32)] * 2
        + [pltpu.VMEM((group_rows, window_rows), bf16)] * 2
        + [pltpu.VMEM((block, query_width), f32), pltpu.VMEM((2, spans, block, pair_width), bf16)],
        [ff_kept],
    )
    held = (query_width // 32, 32, part + spare)
    [ff_grad] = call(
        feed_join_kernel,
        [((3, part, ff_cols), bf16)],
        [places, ff_kept, swap(ff_give, "row", 1)],
        [SMEM, VMEM, VMEM],
        [pltpu.VMEM((3, part, 2 * ff_half), bf16)],
        [pair_own],
    )
    ff_come = over_groups_start(ff_grad)
    partial1, query_mine, query_away = call(
        tail_query_kernel,
        [((block, width), f32)] + [((2 * held[0], *held[1:]), bf16)] * 2,
        [
            inputs_low,
            gains,
            query_a,
            query_b,
            other_normed1,
            swap(after(query_a, *layer_out[1:]), "row", 1),
            swap(query_b, "row", 1),
            middle_low,
            attended,
            swap(after(other_low, pair_own), "row", 1),
            other_attended,
            *qkv_all,
        ],
    )

    pair_mine, pair_away = call(
        add_halves_kernel,
        [(pair_own.shape[1:], bf16)] * 2,
        [pair_own, swap(pair_near1, "row", 1), swap(pair_near3, "row", 1)],
        None,
        (),
        [query_mine],
    )
    pair_come = swap(pair_away, "row", 2)
    pair_sums = pair_mine.astype(f32) + pair_come.astype(f32)
    pair_back = [
        shifted(kept(pair_sums[back]), "col", -back)
        for back in range(1, spans)
    ]

    *results, pair_w_near, pair_w_own = call(
        tail_pair_kernel,
        [((2, block, part), bf16)] * 4 + [((2, pair_width // 32 + 1, 32, part + spare), bf16)] * 2,
        [
            inputs_low,
            gains,
            grad_middle,
            partial1,
            pair_sums[0],
            *pair_back,
            *qkv_all,
            gain2_sums,
            cosine,
            sine,
            middle,
            *layer_out,
        ],
        None,
        (),
        [query_away],
    )
    cut = qkv_cols // 32
    piece = (cut + held[0] // col_count, *held[1:])
    query_pieces = exchange_col(
        call(
            split_kernel,
            [(piece, bf16)] * 4,
            [places, query_mine, swap(query_away, "row", 2)],
            [SMEM, VMEM, VMEM],
            [pltpu.VMEM((4, *piece), bf16)],
            [pair_w_near, ff_come],
        )
    )
    pair_w_mine = scatter_far(*near_sum(pair_w_near, pair_w_own, [query_pieces[0]]))
    pair_low = kept(pair_w_mine)
    pair_w_grad = add_pieces(gather_col(pair_low))
    query_grad = add_pieces(query_pieces)
    results = exchange_row(all_after(results, kept(query_grad)))
    results = jnp.concatenate(_in_order(results, row_place), 1)

    ff_grad = over_groups_end(ff_grad, ff_come)
    gate_grad, up_grad, down_grad = ff_grad[0], ff_grad[1], ff_grad[2]
    out_w_grad = over_groups(query_grad[cut:]).reshape(-1, part + spare)[:, :part]
    last = jnp.where(col_place == col_count - 1, 1.0, 0.0)
    pair_blocks = pair_width // 32
    qkv_grad = query_grad[:cut] + last * jnp.pad(
        pair_w_grad[:pair_blocks], ((cut - pair_blocks, 0), (0, 0), (0, 0))
    )
    qkv_grad = kept(jnp.concatenate([qkv_grad, pair_w_grad[pair_blocks:]], 0))
    qkv_grad = over_groups(qkv_grad)
    qkv_grad = qkv_grad.reshape(-1, part + spare)

    return (
        results[1],
        results[0].astype(f32),
        qkv_grad[qkv_cols, :part],
        qkv_grad[:qkv_cols, :part].T,
        qkv_grad[:qkv_cols, part],
        out_w_grad,
        qkv_grad[qkv_cols + 1, :part],
        gate_grad,
        up_grad,
        down_grad.T,
    )


def _in_order(blocks, place):
    stacked = jnp.stack(blocks, 0)
    return [pick(stacked, place ^ k) for k in range(len(blocks))]


def solution(mesh):
    return jax.shard_map(
        body,
        mesh=mesh,
        in_specs=(
            P(("dp", "col"), "row"),
            P("row"),
            P("row", "col"),
            P("col"),
            P("col", "row"),
            P("row"),
            P("row", "col"),
            P("row", "col"),
            P("col", "row"),
            P("dp", None),
            P(("dp", "col"), "row"),
        ),
        out_specs=(
            P(("dp", "col"), "row"),
            P(("dp", "col"), "row"),
            P("row"),
            P("row", "col"),
            P("col"),
            P("col", "row"),
            P("row"),
            P("row", "col"),
            P("row", "col"),
            P("col", "row"),
        ),
        check_vma=False,
    )
```
